512 devices in a mesh: gx: 8 (over x, core), gy: 8 (over z), gz: 8 (over y).
Axes of the slice: x: 4, y: 8, z: 8, core: 2. Of those that a mesh axis runs over, the one named last changes fastest.
Arguments:
- phase_field: int32 [64, 128, 1024], P('gz', 'gx', 'gy'), may hold values 0 or 1
- thermal: float32 [64, 128, 1024], P('gz', 'gx', 'gy'), may hold values from 0.5 to 1.5
- velocity: float32 [3, 64, 128, 1024], P(None, 'gz', 'gx', 'gy'), may hold values from -6 to 6
- transfer_slope: float32 [8, 4], replicated, may hold values from -3 to 3
- transfer_offset: float32 [8, 4], replicated, may hold values from -1 to 1
- transfer_gain: float32 [8], replicated, may hold values from 0.5 to 4
Outputs:
- corrected: float32 [3, 64, 128, 1024], P(None, 'gz', 'gx', 'gy')
- images: float32 [8, 4, 128, 1024], P('gz', None, 'gx', 'gy')
The draws below stay inside these ranges and needn't reach their ends.
All inputs are finite; a program needn't handle non-finite values. No bound on the sum of `phase_field` on one device may be relied on, other than what follows from the above.
Results may differ from the reference program's by a relative error of at most 0.0001.
Values sent between devices are 32-bit elements; how exact they have to be, the bound alone decides.
A program may use at most 64 MiB of HBM per device.

```python
import math
import jax
import jax.numpy as jnp
from jax import lax

ITERS = 4
TF = 8
NZ = 64
NX = 128
NY = 1024


def touch_ends(drawn, key, low, largest):
    longest = drawn.shape.index(max(drawn.shape))
    spots = []
    for shift in (0, 1):
        where = [jax.random.randint(jax.random.fold_in(key, axis), (), 0, length) for axis, length in enumerate(drawn.shape)]
        where[longest] = (where[longest] + shift) % drawn.shape[longest]
        spots.append(tuple(where))
    return drawn.at[spots[0]].set(low).at[spots[1]].set(largest)


def shard_levels(key, extent, pieces, low, largest):
    level, own = 1.0, jax.random.fold_in(key, 6)
    for position, parts in pieces:
        heights = jnp.exp(jax.random.uniform(jax.random.fold_in(own, position), (parts,), jnp.float32, low / len(pieces), largest / len(pieces)))
        level = level * jnp.repeat(heights, extent[position] // parts).reshape([-1 if axis == position else 1 for axis in range(len(extent))])
    return level


def noise(stream_key, shape, width, most, pieces=(), held_as=jnp.bfloat16):
    level = shard_levels(stream_key, shape, pieces, -0.22, 0.18) if pieces else 1.0
    result = jax.random.normal(stream_key, shape, jnp.float32) * width * level
    return jnp.minimum(jnp.maximum(result, -most), most).astype(held_as)


def setup_inputs(seed: int = 0) -> dict:
    arg_keys = jax.random.split(jax.random.key(seed), 7)
    return {
        "phase_field": touch_ends((jax.random.randint(arg_keys[0], (NZ, NX, NY), 0, 3) < 1).astype(jnp.int32), jax.random.fold_in(arg_keys[0], 1), 0, 1),
        "thermal": jnp.clip(1.0 + 0.1 * jax.random.normal(arg_keys[1], (NZ, NX, NY), jnp.float32), 0.5, 1.5),
        "velocity": noise(arg_keys[2], (3, NZ, NX, NY), 1.0, 6.0, ((1, 8), (2, 8), (3, 8)), jnp.float32),
        "transfer_slope": jnp.clip(jax.random.uniform(arg_keys[3], (TF, 4), jnp.float32, -3.0, 3.0), -3.0, 3.0),
        "transfer_offset": jnp.clip(jax.random.uniform(arg_keys[4], (TF, 4), jnp.float32, -1.0, 1.0), -1.0, 1.0),
        "transfer_gain": jnp.clip(jnp.exp(jax.random.uniform(arg_keys[5], (TF,), jnp.float32, math.log(0.5), math.log(4.0))), 0.5, 4.0),
    }


def below_zero(field, axis):
    edge = jnp.zeros_like(lax.slice_in_dim(field, 0, 1, axis=axis))
    return jnp.concatenate([edge, lax.slice_in_dim(field, 0, field.shape[axis] - 1, axis=axis)], axis=axis)


def above_zero(field, axis):
    edge = jnp.zeros_like(lax.slice_in_dim(field, 0, 1, axis=axis))
    return jnp.concatenate([lax.slice_in_dim(field, 1, field.shape[axis], axis=axis), edge], axis=axis)


def below_edge(field, axis):
    edge = lax.slice_in_dim(field, 0, 1, axis=axis)
    return jnp.concatenate([edge, lax.slice_in_dim(field, 0, field.shape[axis] - 1, axis=axis)], axis=axis)


def above_edge(field, axis):
    count = field.shape[axis]
    edge = lax.slice_in_dim(field, count - 1, count, axis=axis)
    return jnp.concatenate([lax.slice_in_dim(field, 1, count, axis=axis), edge], axis=axis)


def reference(phase_field, thermal, velocity, transfer_slope, transfer_offset, transfer_gain):
    density = (1.0 + 9.0 * phase_field.astype(jnp.float32)) * thermal
    lowers = [2.0 / (density + below_edge(density, which)) for which in range(3)]
    uppers = [2.0 / (density + above_edge(density, which)) for which in range(3)]
    inverse = 1.0 / (lowers[0] + uppers[0] + lowers[1] + uppers[1] + lowers[2] + uppers[2])

    def operate(field):
        total = jnp.zeros_like(field)
        for which in range(3):
            total = total + lowers[which] * (field - below_zero(field, which))
            total = total + uppers[which] * (field - above_zero(field, which))
        return total

    rhs = jnp.zeros_like(density)
    for which in range(3):
        rhs = rhs - (above_zero(velocity[which], which) - velocity[which])
    pressure = jnp.zeros_like(rhs)
    residual = rhs
    precond = inverse * residual
    direction = precond
    norm_now = jnp.sum(residual * precond)
    for iteration in range(ITERS):
        image = operate(direction)
        alpha = norm_now / jnp.sum(direction * image)
        pressure = pressure + alpha * direction
        residual = residual - alpha * image
        if iteration + 1 < ITERS:
            precond = inverse * residual
            norm_next = jnp.sum(residual * precond)
            direction = precond + (norm_next / norm_now) * direction
            norm_now = norm_next
    corrected = jnp.stack([velocity[which] - lowers[which] * (pressure - below_zero(pressure, which)) for which in range(3)])
    scalar = corrected[0] + corrected[1] + corrected[2]

    def render(index):
        slope = transfer_slope[index]
        offset = transfer_offset[index]
        opacity = transfer_gain[index] / NZ * jax.nn.sigmoid(slope[3] * scalar + offset[3])
        keep = 1.0 - opacity
        inclusive = jnp.cumprod(keep, axis=0)
        passed = jnp.concatenate([jnp.ones_like(inclusive[:1]), inclusive[:-1]], axis=0)
        weight = passed * opacity
        planes = [jnp.sum(weight * jax.nn.sigmoid(slope[channel] * scalar + offset[channel]), axis=0) for channel in range(3)]
        planes.append(1.0 - inclusive[-1])
        return jnp.stack(planes)

    images = lax.map(render, jnp.arange(transfer_slope.shape[0]))
    return corrected, images
```

```python
import functools

import jax
import jax.numpy as jnp
from jax import lax
from jax.experimental import pallas as pl
from jax.experimental.pallas import tpu as pltpu
from jax.sharding import PartitionSpec as P

MESH = pl.DeviceIdType.MESH
Z, X, Y = 8, 16, 128
R = Z * X
K = R // 8
TF = 8
PAD = 8
FAR_FIRST = (4, 3, 5, 2, 6, 1, 7)


def lanes(shape):
    return lax.broadcasted_iota(jnp.int32, shape, 1)


def group(v, k):
    return v[8 * k : 8 * k + 8]


def recip(v):
    r = pl.reciprocal(v, approx=True)
    r = r * (2.0 - v * r)
    return r * (2.0 - v * r)


def pack_ends(v):
    lane = lanes((8, Y))
    out = jnp.zeros((8, Y), jnp.float32)
    for k in range(K):
        out = jnp.where(lane // 2 == k, pltpu.roll(group(v, k), 2 * k + 1, 1), out)
    return out


def unpack_ends(below, above):
    lane = lanes((8, Y))
    both = jnp.where(lane % 2 == 0, pltpu.roll(above, Y - 1, 1), pltpu.roll(below, 1, 1))
    return jnp.concatenate([pltpu.roll(both, Y - (2 * k + 1), 1) for k in range(K)], axis=0)


def spread(below, above):
    pieces = []
    for z in range(Z):
        pieces.append(jnp.broadcast_to(below[z : z + 1], (8, Y)))
        pieces.append(jnp.broadcast_to(above[z : z + 1], (8, Y)))
    return jnp.concatenate(pieces, axis=0)


def kernel(
    sizes,
    phase_in,
    thermal_in,
    vel_in,
    slope,
    offset,
    gain,
    corrected,
    images,
    phase_v,
    thermal_v,
    vel_v,
    vel1_pad,
    den_pad,
    s1z,
    s1x,
    s1xu,
    s1y,
    h1,
    v_pad,
    coef,
    edge_z,
    sx,
    sy,
    h,
    grads,
    row_send,
    row_recv,
    scal_v,
    scal_send,
    scal_recv,
    img_send,
    img_recv,
    in_sem,
    send_sem,
    recv_sem,
):
    nx, ny, nz = sizes
    ix, iy, iz = lax.axis_index("gx"), lax.axis_index("gy"), lax.axis_index("gz")
    xm, xp = {"gx": lax.rem(ix + nx - 1, nx)}, {"gx": lax.rem(ix + 1, nx)}
    ym, yp = {"gy": lax.rem(iy + ny - 1, ny)}, {"gy": lax.rem(iy + 1, ny)}
    zm, zp = {"gz": lax.rem(iz + nz - 1, nz)}, {"gz": lax.rem(iz + 1, nz)}
    x_first, x_last = ix == 0, ix == nx - 1
    y_first, y_last = iy == 0, iy == ny - 1
    z_first, z_last = iz == 0, iz == nz - 1

    loads = [
        pltpu.make_async_copy(phase_in, phase_v, in_sem.at[0]),
        pltpu.make_async_copy(thermal_in, thermal_v, in_sem.at[1]),
        pltpu.make_async_copy(vel_in, vel_v, in_sem.at[2]),
    ]
    for copy in loads:
        copy.start()

    barrier = pltpu.get_barrier_semaphore()
    greeted = 0
    for name, here, count in (("gx", ix, nx), ("gy", iy, ny), ("gz", iz, nz)):
        for k in range(1, count):
            pl.semaphore_signal(
                barrier, inc=1, device_id={name: lax.rem(here + k, count)}, device_id_type=MESH
            )
            greeted += 1

    pad = jnp.zeros((PAD, Y), jnp.float32)
    for ref in [den_pad, vel1_pad] + [v_pad.at[j] for j in range(4)]:
        ref[0:PAD] = pad
        ref[PAD + R : PAD + R + PAD] = pad

    def send(src, dst, group_id, device):
        pltpu.make_async_remote_copy(
            src, dst, send_sem.at[group_id], recv_sem.at[group_id], device_id=device, device_id_type=MESH
        ).start()

    def whole(ref, group_id):
        return pltpu.make_async_remote_copy(
            ref, ref, send_sem.at[group_id], recv_sem.at[group_id], device_id=xp, device_id_type=MESH
        )

    lane = lanes((R, Y))
    row = lax.broadcasted_iota(jnp.int32, (R, Y), 0)
    in_x = row % X

    for copy in loads:
        copy.wait()
    den = (1.0 + 9.0 * phase_v[...].astype(jnp.float32)) * thermal_v[...]
    den_pad[PAD : PAD + R] = den
    vel0, vel1, vel2 = vel_v[0:R], vel_v[R : 2 * R], vel_v[2 * R : 3 * R]
    vel1_pad[PAD : PAD + R] = vel1
    s1z[0:X] = den[0:X]
    s1z[X : 2 * X] = vel0[0:X]
    s1x[0:8] = den_pad[pl.ds(PAD, 8, stride=X)]
    s1x[8:16] = vel1_pad[pl.ds(PAD, 8, stride=X)]
    s1xu[...] = den_pad[pl.ds(PAD + X - 1, 8, stride=X)]
    ends = pack_ends(den)
    lane8 = lanes((8, Y))
    for k in range(K):
        ends = jnp.where(lane8 == 2 * K + k, pltpu.roll(group(vel2, k), 2 * K + k, 1), ends)
    s1y[...] = ends

    pl.semaphore_wait(barrier, greeted)

    send(den_pad.at[pl.ds(PAD + R - X, X)], h1.at[pl.ds(0, 16)], 0, zp)
    send(s1z, h1.at[pl.ds(16, 32)], 0, zm)
    send(s1xu, h1.at[pl.ds(48, 8)], 0, xp)
    send(s1x, h1.at[pl.ds(56, 16)], 0, xm)
    send(s1y, h1.at[pl.ds(72, 8)], 0, yp)
    send(s1y, h1.at[pl.ds(80, 8)], 0, ym)
    whole(h1, 0).wait_recv()

    def face(first, own, other):
        return jnp.where(first, own, other)

    zb = jnp.concatenate([face(z_first, den[0:X], h1[0:16]), den[: R - X]], axis=0)
    za = jnp.concatenate([den[X:], face(z_last, den[R - X :], h1[16:32])], axis=0)
    bx = spread(h1[48:56], h1[56:64])
    xb = jnp.where(in_x == 0, face(x_first, den, bx), den_pad[PAD - 1 : PAD - 1 + R])
    xa = jnp.where(in_x == X - 1, face(x_last, den, bx), den_pad[PAD + 1 : PAD + 1 + R])
    by = unpack_ends(h1[72:80], h1[80:88])
    yb = jnp.where(lane == 0, face(y_first, den, by), pltpu.roll(den, 1, 1))
    ya = jnp.where(lane == Y - 1, face(y_last, den, by), pltpu.roll(den, Y - 1, 1))
    low_z, up_z = 2.0 * recip(den + zb), 2.0 * recip(den + za)
    low_x, up_x = 2.0 * recip(den + xb), 2.0 * recip(den + xa)
    low_y, up_y = 2.0 * recip(den + yb), 2.0 * recip(den + ya)
    inverse = recip(low_z + up_z + low_x + up_x + low_y + up_y)

    def keep(flag):
        return jnp.where(flag, 0.0, 1.0)

    zero = jnp.zeros((R, Y), jnp.float32)
    coef[0] = low_z
    coef[1] = low_x
    coef[2] = low_y
    coef[3] = up_z
    coef[4] = jnp.where(in_x == X - 1, 0.0, up_x)
    coef[5] = jnp.where(lane == Y - 1, 0.0, up_y)
    coef[6] = jnp.where(in_x == 0, 0.0, low_x)
    coef[7] = jnp.where(lane == 0, 0.0, low_y)
    coef[8] = jnp.where(
        in_x == 0, low_x * keep(x_first), jnp.where(in_x == X - 1, up_x * keep(x_last), zero)
    )
    coef[9] = jnp.where(
        lane == 0, low_y * keep(y_first), jnp.where(lane == Y - 1, up_y * keep(y_last), zero)
    )
    coef[10] = inverse
    edge_z[0:X] = low_z[0:X] * keep(z_first)
    edge_z[X : 2 * X] = up_z[R - X :] * keep(z_last)

    above0 = jnp.concatenate([vel0[X:], h1[32:48] * keep(z_last)], axis=0)
    bv = spread(h1[56:64], h1[64:72])
    above1 = jnp.where(in_x == X - 1, bv * keep(x_last), vel1_pad[PAD + 1 : PAD + 1 + R])
    ends_above = h1[80:88]
    bw = jnp.concatenate(
        [pltpu.roll(ends_above, Y - 1 - (2 * K + k), 1) for k in range(K)], axis=0
    )
    above2 = jnp.where(lane == Y - 1, bw * keep(y_last), pltpu.roll(vel2, Y - 1, 1))
    rhs = -(((above0 - vel0) + (above1 - vel1)) + (above2 - vel2))

    def total(v):
        return jnp.sum(v.reshape(K, 8, Y), axis=0)

    sums = []
    scaled = rhs
    for j in range(4):
        v = coef[10] * scaled
        own = v_pad.at[j]
        own[PAD : PAD + R] = v
        sx[j, 0:8] = own[pl.ds(PAD, 8, stride=X)]
        sx[j, 8:16] = own[pl.ds(PAD + X - 1, 8, stride=X)]
        sy[j] = pack_ends(v)
        hj = h.at[j]
        send(own.at[pl.ds(PAD + R - X, X)], hj.at[pl.ds(0, 16)], 1 + j, zp)
        send(own.at[pl.ds(PAD, X)], hj.at[pl.ds(16, 16)], 1 + j, zm)
        send(sx.at[j, pl.ds(8, 8)], hj.at[pl.ds(32, 8)], 1 + j, xp)
        send(sx.at[j, pl.ds(0, 8)], hj.at[pl.ds(40, 8)], 1 + j, xm)
        send(sy.at[j], hj.at[pl.ds(48, 8)], 1 + j, yp)
        send(sy.at[j], hj.at[pl.ds(56, 8)], 1 + j, ym)

        sums.append(total(scaled * v))
        z_low = coef[0, X:R] * v[: R - X]
        z_up = coef[3, 0 : R - X] * v[X:]
        x_low = coef[6] * own[PAD - 1 : PAD - 1 + R]
        x_up = coef[4] * own[PAD + 1 : PAD + 1 + R]
        y_low = coef[7] * pltpu.roll(v, 1, 1)
        y_up = coef[5] * pltpu.roll(v, Y - 1, 1)
        rest = (x_low + x_up) + (y_low + y_up)

        whole(hj, 1 + j).wait_recv()
        z_low = jnp.concatenate([edge_z[0:X] * hj[0:16], z_low], axis=0)
        z_up = jnp.concatenate([z_up, edge_z[X : 2 * X] * hj[16:32]], axis=0)
        x_edge = coef[8] * spread(hj[32:40], hj[40:48])
        y_edge = coef[9] * unpack_ends(hj[48:56], hj[56:64])
        image = ((z_low + z_up) + rest) + (x_edge + y_edge)
        sums.append(total(v * image))

        g0 = coef[0] * v - z_low
        g1 = coef[1] * v - x_low - jnp.where(in_x == 0, x_edge, 0.0)
        g2 = coef[2] * v - y_low - jnp.where(lane == 0, y_edge, 0.0)
        grads[j, 0] = g0
        grads[j, 1] = g1
        grads[j, 2] = g2
        grads[j, 3] = g0 + g1 + g2
        scaled = image

    folded = jnp.zeros((8, Y), jnp.float32)
    for m, value in enumerate(sums):
        value = value + pltpu.roll(value, 64, 1)
        value = value + pltpu.roll(value, 32, 1)
        value = value + pltpu.roll(value, 16, 1)
        folded = jnp.where(lane8 // 16 == m, value, folded)
    line = jnp.sum(folded, axis=0, keepdims=True)
    for stage, (name, here, count) in enumerate((("gx", ix, nx), ("gy", iy, ny), ("gz", iz, nz))):
        row_send[stage] = line
        for k in FAR_FIRST:
            if k < count:
                send(
                    row_send.at[stage],
                    row_recv.at[stage, k - 1],
                    5 + stage,
                    {name: lax.rem(here + k, count)},
                )
        whole(row_recv.at[stage, pl.ds(0, count - 1)], 5 + stage).wait_recv()
        for k in range(count - 1):
            line = line + row_recv[stage, k]
    lane1 = lanes((1, Y))
    m = [jnp.sum(jnp.where(lane1 // 16 == i, line, 0.0), axis=1, keepdims=True) for i in range(8)]

    a = [[m[i + j] - m[i + j + 1] for j in range(4)] for i in range(4)]
    b = [m[i] for i in range(4)]
    pivots = []
    for p in range(4):
        ok = a[p][p] > 1e-7 * (m[2 * p] - m[2 * p + 1])
        pivots.append(jnp.where(ok, 1.0 / jnp.where(ok, a[p][p], 1.0), 0.0))
        for i in range(p + 1, 4):
            factor = a[p][i] * pivots[p]
            for j in range(i, 4):
                a[i][j] = a[i][j] - factor * a[p][j]
            b[i] = b[i] - factor * b[p]
    c = [None] * 4
    for p in reversed(range(4)):
        value = b[p]
        for j in range(p + 1, 4):
            value = value - a[p][j] * c[j]
        c[p] = value * pivots[p]

    vel = [vel_v[d * R : (d + 1) * R] for d in range(3)]
    scalar = vel[0] + vel[1] + vel[2]
    for j in range(4):
        scalar = scalar - c[j] * grads[j, 3]
    scal_v[...] = scalar
    for t in range(TF):
        scal_send[t, 0:8] = scal_v[pl.ds(t, 8, stride=8)]
        scal_send[t, 8:16] = scal_v[pl.ds(R // 2 + t, 8, stride=8)]
    for k in FAR_FIRST:
        to = lax.rem(iz + k, nz)
        send(scal_send.at[to], scal_recv.at[pl.ds(iz * 16, 16)], 8, {"gz": to})
    scal_recv[pl.ds(pl.multiple_of(iz * 16, 16), 16)] = scal_send[iz]
    for d in range(3):
        value = vel[d]
        for j in range(4):
            value = value - c[j] * grads[j, d]
        corrected[d * R : (d + 1) * R] = value
    whole(scal_recv.at[pl.ds(0, 16 * (nz - 1))], 8).wait_recv()

    field = [
        jnp.concatenate([scal_recv[pl.ds(2 * z + r, 8, stride=16)] for r in range(2)], axis=0)
        for z in range(Z)
    ]
    sub = lax.broadcasted_iota(jnp.int32, (8, Y), 0)
    for k in FAR_FIRST + (0,):
        t = lax.rem(iz + k, nz)
        half = 0.5 / (Z * nz) * gain[t]
        slopes = [0.5 * slope[t, i] for i in range(4)]
        offsets = [0.5 * offset[t, i] for i in range(4)]
        through = jnp.ones((16, Y), jnp.float32)
        colors = [jnp.zeros((16, Y), jnp.float32) for _ in range(3)]
        for z in range(Z):
            weight = through * (half + half * jnp.tanh(slopes[3] * field[z] + offsets[3]))
            through = through - weight
            for i in range(3):
                colors[i] = colors[i] + weight * jnp.tanh(slopes[i] * field[z] + offsets[i])
        lines = [[None, None] for _ in range(4)]
        for r in range(2):
            here = through[8 * r : 8 * r + 8]
            before = jnp.where(sub >= 1, pltpu.roll(here, 1, 0), 1.0)
            for step in (1, 2, 4):
                before = before * jnp.where(sub >= step, pltpu.roll(before, step, 0), 1.0)
            for i in range(3):
                color = 0.5 * (colors[i][8 * r : 8 * r + 8] + (1.0 - here))
                lines[i][r] = jnp.sum(before * color, axis=0, keepdims=True)
            lines[3][r] = (1.0 - before * here)[7:8]
        tile = jnp.concatenate([lines[i][r] for i in range(4) for r in range(2)], axis=0)
        if k:
            img_send[t] = tile
            send(img_send.at[t], img_recv.at[pl.ds(iz * 8, 8)], 9, {"gz": t})
        else:
            img_recv[pl.ds(pl.multiple_of(iz * 8, 8), 8)] = tile
    whole(img_recv.at[pl.ds(0, 8 * (nz - 1))], 9).wait_recv()
    for i in range(4):
        for r in range(2):
            images[i * X + 8 * r : i * X + 8 * r + 8] = img_recv[pl.ds(2 * i + r, 8, stride=8)]

    whole(h1, 0).wait_send()
    for j in range(4):
        whole(h.at[j], 1 + j).wait_send()
    for stage, count in enumerate((nx, ny, nz)):
        whole(row_recv.at[stage, pl.ds(0, count - 1)], 5 + stage).wait_send()
    whole(scal_recv.at[pl.ds(0, 16 * (nz - 1))], 8).wait_send()
    whole(img_recv.at[pl.ds(0, 8 * (nz - 1))], 9).wait_send()


def local(sizes, phase_field, thermal, velocity, transfer_slope, transfer_offset, transfer_gain):
    f32 = jnp.float32
    hbm = pl.BlockSpec(memory_space=pl.ANY)
    smem = pl.BlockSpec(memory_space=pltpu.SMEM)
    vmem = pl.BlockSpec(memory_space=pltpu.VMEM)
    corrected, images = pl.pallas_call(
        functools.partial(kernel, sizes),
        out_shape=(
            jax.ShapeDtypeStruct((3 * R, Y), f32),
            jax.ShapeDtypeStruct((4 * X, Y), f32),
        ),
        in_specs=[hbm, hbm, hbm, smem, smem, smem],
        out_specs=(vmem, vmem),
        scratch_shapes=[
            pltpu.VMEM((R, Y), jnp.int32),
            pltpu.VMEM((R, Y), f32),
            pltpu.VMEM((3 * R, Y), f32),
            pltpu.VMEM((R + 2 * PAD, Y), f32),
            pltpu.VMEM((R + 2 * PAD, Y), f32),
            pltpu.VMEM((2 * X, Y), f32),
            pltpu.VMEM((16, Y), f32),
            pltpu.VMEM((8, Y), f32),
            pltpu.VMEM((8, Y), f32),
            pltpu.VMEM((88, Y), f32),
            pltpu.VMEM((4, R + 2 * PAD, Y), f32),
            pltpu.VMEM((11, R, Y), f32),
            pltpu.VMEM((2 * X, Y), f32),
            pltpu.VMEM((4, 16, Y), f32),
            pltpu.VMEM((4, 8, Y), f32),
            pltpu.VMEM((4, 64, Y), f32),
            pltpu.VMEM((4, 4, R, Y), f32),
            pltpu.VMEM((3, 1, Y), f32),
            pltpu.VMEM((3, 7, 1, Y), f32),
            pltpu.VMEM((R, Y), f32),
            pltpu.VMEM((TF, 16, Y), f32),
            pltpu.VMEM((TF * 16, Y), f32),
            pltpu.VMEM((TF, 8, Y), f32),
            pltpu.VMEM((TF * 8, Y), f32),
            pltpu.SemaphoreType.DMA((3,)),
            pltpu.SemaphoreType.DMA((10,)),
            pltpu.SemaphoreType.DMA((10,)),
        ],
        compiler_params=pltpu.CompilerParams(
            collective_id=0, has_side_effects=True, vmem_limit_bytes=16 * 2**20
        ),
    )(
        phase_field.reshape(R, Y),
        thermal.reshape(R, Y),
        velocity.reshape(3 * R, Y),
        transfer_slope,
        transfer_offset,
        transfer_gain,
    )
    return corrected.reshape(3, Z, X, Y), images.reshape(1, 4, X, Y)


def solution(mesh):
    sizes = (mesh.shape["gx"], mesh.shape["gy"], mesh.shape["gz"])
    return jax.shard_map(
        functools.partial(local, sizes),
        mesh=mesh,
        in_specs=(
            P("gz", "gx", "gy"),
            P("gz", "gx", "gy"),
            P(None, "gz", "gx", "gy"),
            P(),
            P(),
            P(),
        ),
        out_specs=(P(None, "gz", "gx", "gy"), P("gz", None, "gx", "gy")),
        check_vma=False,
    )
```

```python
import functools

import jax
import jax.numpy as jnp
from jax import lax
from jax.experimental import pallas as pl
from jax.experimental.pallas import tpu as pltpu
from jax.sharding import PartitionSpec as P

MESH = pl.DeviceIdType.MESH
Z, X, Y = 8, 16, 128
R = Z * X
K = R // 8
TF = 8
PAD = 8
FAR_FIRST = (4, 3, 5, 2, 6, 1, 7)


def lanes(shape):
    return lax.broadcasted_iota(jnp.int32, shape, 1)


def group(v, k):
    return v[8 * k : 8 * k + 8]


def recip(v):
    r = pl.reciprocal(v, approx=True)
    r = r * (2.0 - v * r)
    return r * (2.0 - v * r)


def pack_ends(v):
    lane = lanes((8, Y))
    out = jnp.zeros((8, Y), jnp.float32)
    for k in range(K):
        out = jnp.where(lane // 2 == k, pltpu.roll(group(v, k), 2 * k + 1, 1), out)
    return out


def unpack_ends(below, above):
    lane = lanes((8, Y))
    both = jnp.where(lane % 2 == 0, pltpu.roll(above, Y - 1, 1), pltpu.roll(below, 1, 1))
    return jnp.concatenate([pltpu.roll(both, Y - (2 * k + 1), 1) for k in range(K)], axis=0)


def spread(below, above):
    pieces = []
    for z in range(Z):
        pieces.append(jnp.broadcast_to(below[z : z + 1], (8, Y)))
        pieces.append(jnp.broadcast_to(above[z : z + 1], (8, Y)))
    return jnp.concatenate(pieces, axis=0)


def kernel(
    sizes,
    phase_in,
    thermal_in,
    vel_in,
    slope_in,
    offset_in,
    gain_in,
    corrected,
    images,
    slope,
    offset,
    gain,
    phase_v,
    thermal_v,
    vel_v,
    vel1_pad,
    den_pad,
    s1z,
    s1x,
    s1xu,
    s1y,
    h1,
    v_pad,
    coef,
    edge_z,
    sx,
    sy,
    h,
    grads,
    row_send,
    row_recv,
    send_a,
    send_b,
    send_c,
    recv_a,
    recv_b,
    recv_c,
    vel_sum,
    img_send,
    img_recv,
    in_sem,
    send_sem,
    recv_sem,
):
    nx, ny, nz = sizes
    ix, iy, iz = lax.axis_index("gx"), lax.axis_index("gy"), lax.axis_index("gz")
    xm, xp = {"gx": lax.rem(ix + nx - 1, nx)}, {"gx": lax.rem(ix + 1, nx)}
    ym, yp = {"gy": lax.rem(iy + ny - 1, ny)}, {"gy": lax.rem(iy + 1, ny)}
    zm, zp = {"gz": lax.rem(iz + nz - 1, nz)}, {"gz": lax.rem(iz + 1, nz)}
    x_first, x_last = ix == 0, ix == nx - 1
    y_first, y_last = iy == 0, iy == ny - 1
    z_first, z_last = iz == 0, iz == nz - 1

    loads = [
        pltpu.make_async_copy(phase_in, phase_v, in_sem.at[0]),
        pltpu.make_async_copy(thermal_in, thermal_v, in_sem.at[1]),
        pltpu.make_async_copy(vel_in, vel_v, in_sem.at[2]),
    ]
    params = [
        pltpu.make_async_copy(slope_in, slope, in_sem.at[3]),
        pltpu.make_async_copy(offset_in, offset, in_sem.at[4]),
        pltpu.make_async_copy(gain_in, gain, in_sem.at[5]),
    ]
    barrier = pltpu.get_barrier_semaphore()
    for device in (zm, zp, ym, yp, xm, xp):
        pl.semaphore_signal(barrier, inc=1, device_id=device, device_id_type=MESH)
    for copy in loads + params:
        copy.start()

    pad = jnp.zeros((PAD, Y), jnp.float32)
    for ref in [den_pad, vel1_pad] + [v_pad.at[j] for j in range(4)]:
        ref[0:PAD] = pad
        ref[PAD + R : PAD + R + PAD] = pad

    def send(src, dst, group_id, device):
        pltpu.make_async_remote_copy(
            src, dst, send_sem.at[group_id], recv_sem.at[group_id], device_id=device, device_id_type=MESH
        ).start()

    def whole(ref, group_id):
        return pltpu.make_async_remote_copy(
            ref, ref, send_sem.at[group_id], recv_sem.at[group_id], device_id=xp, device_id_type=MESH
        )

    lane = lanes((R, Y))
    row = lax.broadcasted_iota(jnp.int32, (R, Y), 0)
    in_x = row % X

    for copy in loads:
        copy.wait()
    den = (1.0 + 9.0 * phase_v[...].astype(jnp.float32)) * thermal_v[...]
    den_pad[PAD : PAD + R] = den
    vel0, vel1, vel2 = vel_v[0:R], vel_v[R : 2 * R], vel_v[2 * R : 3 * R]
    vel1_pad[PAD : PAD + R] = vel1
    s1z[0:X] = den[0:X]
    s1z[X : 2 * X] = vel0[0:X]
    s1x[0:8] = den_pad[pl.ds(PAD, 8, stride=X)]
    s1x[8:16] = vel1_pad[pl.ds(PAD, 8, stride=X)]
    s1xu[...] = den_pad[pl.ds(PAD + X - 1, 8, stride=X)]
    ends = pack_ends(den)
    lane8 = lanes((8, Y))
    for k in range(K):
        ends = jnp.where(lane8 == 2 * K + k, pltpu.roll(group(vel2, k), 2 * K + k, 1), ends)
    s1y[...] = ends

    pl.semaphore_wait(barrier, 6)

    send(den_pad.at[pl.ds(PAD + R - X, X)], h1.at[pl.ds(0, 16)], 0, zp)
    send(s1z, h1.at[pl.ds(16, 32)], 0, zm)
    send(s1xu, h1.at[pl.ds(48, 8)], 0, xp)
    send(s1x, h1.at[pl.ds(56, 16)], 0, xm)
    send(s1y, h1.at[pl.ds(72, 8)], 0, yp)
    send(s1y, h1.at[pl.ds(80, 8)], 0, ym)
    whole(h1, 0).wait_recv()

    def face(first, own, other):
        return jnp.where(first, own, other)

    zb = jnp.concatenate([face(z_first, den[0:X], h1[0:16]), den[: R - X]], axis=0)
    za = jnp.concatenate([den[X:], face(z_last, den[R - X :], h1[16:32])], axis=0)
    bx = spread(h1[48:56], h1[56:64])
    xb = jnp.where(in_x == 0, face(x_first, den, bx), den_pad[PAD - 1 : PAD - 1 + R])
    xa = jnp.where(in_x == X - 1, face(x_last, den, bx), den_pad[PAD + 1 : PAD + 1 + R])
    by = unpack_ends(h1[72:80], h1[80:88])
    yb = jnp.where(lane == 0, face(y_first, den, by), pltpu.roll(den, 1, 1))
    ya = jnp.where(lane == Y - 1, face(y_last, den, by), pltpu.roll(den, Y - 1, 1))
    low_z, up_z = 2.0 * recip(den + zb), 2.0 * recip(den + za)
    low_x, up_x = 2.0 * recip(den + xb), 2.0 * recip(den + xa)
    low_y, up_y = 2.0 * recip(den + yb), 2.0 * recip(den + ya)
    inverse = recip(low_z + up_z + low_x + up_x + low_y + up_y)

    def keep(flag):
        return jnp.where(flag, 0.0, 1.0)

    zero = jnp.zeros((R, Y), jnp.float32)
    coef[0] = low_z
    coef[1] = low_x
    coef[2] = low_y
    coef[3] = up_z
    coef[4] = jnp.where(in_x == X - 1, 0.0, up_x)
    coef[5] = jnp.where(lane == Y - 1, 0.0, up_y)
    coef[6] = jnp.where(in_x == 0, 0.0, low_x)
    coef[7] = jnp.where(lane == 0, 0.0, low_y)
    coef[8] = jnp.where(
        in_x == 0, low_x * keep(x_first), jnp.where(in_x == X - 1, up_x * keep(x_last), zero)
    )
    coef[9] = jnp.where(
        lane == 0, low_y * keep(y_first), jnp.where(lane == Y - 1, up_y * keep(y_last), zero)
    )
    coef[10] = inverse
    edge_z[0:X] = low_z[0:X] * keep(z_first)
    edge_z[X : 2 * X] = up_z[R - X :] * keep(z_last)

    above0 = jnp.concatenate([vel0[X:], h1[32:48] * keep(z_last)], axis=0)
    bv = spread(h1[56:64], h1[64:72])
    above1 = jnp.where(in_x == X - 1, bv * keep(x_last), vel1_pad[PAD + 1 : PAD + 1 + R])
    ends_above = h1[80:88]
    bw = jnp.concatenate(
        [pltpu.roll(ends_above, Y - 1 - (2 * K + k), 1) for k in range(K)], axis=0
    )
    above2 = jnp.where(lane == Y - 1, bw * keep(y_last), pltpu.roll(vel2, Y - 1, 1))
    rhs = -(((above0 - vel0) + (above1 - vel1)) + (above2 - vel2))

    def hand_out(buf, recv, group_id, steps):
        rows = buf.shape[1]
        for k in steps:
            to = lax.rem(iz + k, nz)
            send(buf.at[to], recv.at[pl.ds(iz * rows, rows)], group_id, {"gz": to})

    def scatter(fields, buf, recv, group_id, steps):
        for q, ref in enumerate(fields):
            for t in range(TF):
                for r in range(2):
                    at = 16 * q + 8 * r
                    buf[t, at : at + 8] = ref[pl.ds(r * (R // 2) + t, 8, stride=8)]
        rows = 16 * len(fields)
        hand_out(buf, recv, group_id, steps)
        recv[pl.ds(pl.multiple_of(iz * rows, rows), rows)] = buf[iz]

    folded = []

    def fold(value):
        value = jnp.sum(value.reshape(K, 8, Y), axis=0)
        for step in (64, 32, 16):
            value = value + pltpu.roll(value, step, 1)
        m = len(folded)
        before = folded[-1] if folded else jnp.zeros((8, Y), jnp.float32)
        folded.append(jnp.where(lane8 // 16 == m, value, before))

    def gradient(j, v, z_low, x_low, y_low):
        g0, g1, g2 = coef[0] * v - z_low, coef[1] * v - x_low, coef[2] * v - y_low
        grads[j, 0] = g0
        grads[j, 1] = g1
        grads[j, 2] = g2
        grads[j, 3] = g0 + g1 + g2

    vel_sum[...] = vel0 + vel1 + vel2
    scaled = rhs
    last = None
    for j in range(4):
        v = coef[10] * scaled
        own = v_pad.at[j]
        own[PAD : PAD + R] = v
        sx[j, 8:16] = own[pl.ds(PAD + X - 1, 8, stride=X)]
        sy[j] = pack_ends(v)
        hj = h.at[j]
        send(own.at[pl.ds(PAD + R - X, X)], hj.at[pl.ds(0, 16)], 1 + j, zp)
        if j < 3:
            send(own.at[pl.ds(PAD, X)], hj.at[pl.ds(32, 16)], 1 + j, zm)
        send(sy.at[j], hj.at[pl.ds(24, 8)], 1 + j, yp)
        if j < 3:
            send(sy.at[j], hj.at[pl.ds(56, 8)], 1 + j, ym)
        send(sx.at[j, pl.ds(8, 8)], hj.at[pl.ds(16, 8)], 1 + j, xp)
        if j < 3:
            sx[j, 0:8] = own[pl.ds(PAD, 8, stride=X)]
            send(sx.at[j, pl.ds(0, 8)], hj.at[pl.ds(48, 8)], 1 + j, xm)

        if j:
            fold(last[0] * last[5])
            gradient(j - 1, last[0], *last[2:5])
        fold(scaled * v)
        z_low = coef[0, X:R] * v[: R - X]
        x_low = coef[6] * own[PAD - 1 : PAD - 1 + R]
        y_low = coef[7] * pltpu.roll(v, 1, 1)
        if j < 3:
            z_up = coef[3, 0 : R - X] * v[X:]
            x_up = coef[4] * own[PAD + 1 : PAD + 1 + R]
            y_up = coef[5] * pltpu.roll(v, Y - 1, 1)
            rest = (x_low + x_up) + (y_low + y_up)
        if j == 1:
            scatter([vel_sum, grads.at[0, 3]], send_a, recv_a, 8, FAR_FIRST[1:])
        if j == 2:
            hand_out(send_a, recv_a, 8, FAR_FIRST[:1])
            scatter([grads.at[1, 3]], send_b, recv_b, 9, FAR_FIRST)

        if j < 3:
            whole(hj, 1 + j).wait_recv()
            z_low = jnp.concatenate([edge_z[0:X] * hj[0:16], z_low], axis=0)
            z_up = jnp.concatenate([z_up, edge_z[X : 2 * X] * hj[32:48]], axis=0)
            x_edge = coef[8] * spread(hj[16:24], hj[48:56])
            y_edge = coef[9] * unpack_ends(hj[24:32], hj[56:64])
            image = ((z_low + z_up) + rest) + (x_edge + y_edge)
            x_low = x_low + jnp.where(in_x == 0, x_edge, 0.0)
            y_low = y_low + jnp.where(lane == 0, y_edge, 0.0)
            last = (v, None, z_low, x_low, y_low, image)
            scaled = image
        else:
            whole(hj.at[pl.ds(0, 32)], 1 + j).wait_recv()
            z_low = jnp.concatenate([edge_z[0:X] * hj[0:16], z_low], axis=0)
            x_edge = coef[8] * spread(hj[16:24], hj[16:24])
            y_edge = coef[9] * unpack_ends(hj[24:32], hj[24:32])
            x_low = x_low + jnp.where(in_x == 0, x_edge, 0.0)
            y_low = y_low + jnp.where(lane == 0, y_edge, 0.0)
            fold((2.0 * v) * ((z_low + x_low) + y_low))

    line = jnp.sum(folded[-1], axis=0, keepdims=True)
    for stage, (name, here, count) in enumerate((("gx", ix, nx), ("gy", iy, ny), ("gz", iz, nz))):
        row_send[stage] = line
        for k in FAR_FIRST:
            if k < count:
                send(
                    row_send.at[stage],
                    row_recv.at[stage, k - 1],
                    5 + stage,
                    {name: lax.rem(here + k, count)},
                )
        if stage == 0:
            gradient(3, v, z_low, x_low, y_low)
            scatter([grads.at[2, 3], grads.at[3, 3]], send_c, recv_c, 10, FAR_FIRST)
        if stage == 2:
            for ref, group_id in ((recv_a, 8), (recv_b, 9), (recv_c, 10)):
                whole(ref.at[pl.ds(0, ref.shape[0] // nz * (nz - 1))], group_id).wait_recv()
            for copy in params:
                copy.wait()
        whole(row_recv.at[stage, pl.ds(0, count - 1)], 5 + stage).wait_recv()
        for k in range(count - 1):
            line = line + row_recv[stage, k]
    lane1 = lanes((1, Y))
    m = [jnp.sum(jnp.where(lane1 // 16 == i, line, 0.0), axis=1, keepdims=True) for i in range(8)]

    a = [[m[i + j] - m[i + j + 1] for j in range(4)] for i in range(4)]
    b = [m[i] for i in range(4)]
    pivots = []
    for p in range(4):
        ok = a[p][p] > 1e-7 * (m[2 * p] - m[2 * p + 1])
        pivots.append(jnp.where(ok, 1.0 / jnp.where(ok, a[p][p], 1.0), 0.0))
        for i in range(p + 1, 4):
            factor = a[p][i] * pivots[p]
            for j in range(i, 4):
                a[i][j] = a[i][j] - factor * a[p][j]
            b[i] = b[i] - factor * b[p]
    c = [None] * 4
    for p in reversed(range(4)):
        value = b[p]
        for j in range(p + 1, 4):
            value = value - a[p][j] * c[j]
        c[p] = value * pivots[p]

    field = []
    for z in range(Z):
        halves = []
        for r in range(2):
            at = 2 * z + r
            value = recv_a[pl.ds(at, 8, stride=32)]
            value = value - c[0] * recv_a[pl.ds(16 + at, 8, stride=32)]
            value = value - c[1] * recv_b[pl.ds(at, 8, stride=16)]
            value = value - c[2] * recv_c[pl.ds(at, 8, stride=32)]
            value = value - c[3] * recv_c[pl.ds(16 + at, 8, stride=32)]
            halves.append(value)
        field.append(jnp.concatenate(halves, axis=0))
    sub = lax.broadcasted_iota(jnp.int32, (8, Y), 0)
    for k in FAR_FIRST + (0,):
        t = lax.rem(iz + k, nz)
        half = 0.5 / (Z * nz) * gain[t]
        slopes = [0.5 * slope[i, t] for i in range(4)]
        offsets = [0.5 * offset[i, t] for i in range(4)]
        through = jnp.ones((16, Y), jnp.float32)
        colors = [jnp.zeros((16, Y), jnp.float32) for _ in range(3)]
        for z in range(Z):
            weight = through * (half + half * jnp.tanh(slopes[3] * field[z] + offsets[3]))
            through = through - weight
            for i in range(3):
                colors[i] = colors[i] + weight * jnp.tanh(slopes[i] * field[z] + offsets[i])
        lines = [[None, None] for _ in range(4)]
        for r in range(2):
            here = through[8 * r : 8 * r + 8]
            before = jnp.where(sub >= 1, pltpu.roll(here, 1, 0), 1.0)
            for step in (1, 2, 4):
                before = before * jnp.where(sub >= step, pltpu.roll(before, step, 0), 1.0)
            for i in range(3):
                color = 0.5 * (colors[i][8 * r : 8 * r + 8] + (1.0 - here))
                lines[i][r] = jnp.sum(before * color, axis=0, keepdims=True)
            lines[3][r] = (1.0 - before * here)[7:8]
        tile = jnp.concatenate([lines[i][r] for i in range(4) for r in range(2)], axis=0)
        if k:
            img_send[t] = tile
            send(img_send.at[t], img_recv.at[pl.ds(iz * 8, 8)], 11, {"gz": t})
        else:
            img_recv[pl.ds(pl.multiple_of(iz * 8, 8), 8)] = tile
    for d in range(3):
        value = vel_v[d * R : (d + 1) * R]
        for j in range(4):
            value = value - c[j] * grads[j, d]
        corrected[d * R : (d + 1) * R] = value
    whole(img_recv.at[pl.ds(0, 8 * (nz - 1))], 11).wait_recv()
    for i in range(4):
        for r in range(2):
            images[i * X + 8 * r : i * X + 8 * r + 8] = img_recv[pl.ds(2 * i + r, 8, stride=8)]

    whole(h1, 0).wait_send()
    for j in range(4):
        whole(h.at[j, pl.ds(0, 64 if j < 3 else 32)], 1 + j).wait_send()
    for stage, count in enumerate((nx, ny, nz)):
        whole(row_recv.at[stage, pl.ds(0, count - 1)], 5 + stage).wait_send()
    for ref, group_id in ((recv_a, 8), (recv_b, 9), (recv_c, 10), (img_recv, 11)):
        whole(ref.at[pl.ds(0, ref.shape[0] // nz * (nz - 1))], group_id).wait_send()


def local(sizes, phase_field, thermal, velocity, transfer_slope, transfer_offset, transfer_gain):
    f32 = jnp.float32
    hbm = pl.BlockSpec(memory_space=pltpu.HBM)
    vmem = pl.BlockSpec(memory_space=pltpu.VMEM)
    corrected, images = pl.pallas_call(
        functools.partial(kernel, sizes),
        out_shape=(
            jax.ShapeDtypeStruct((3 * R, Y), f32),
            jax.ShapeDtypeStruct((4 * X, Y), f32),
        ),
        in_specs=[hbm] * 6,
        out_specs=(vmem, vmem),
        scratch_shapes=[
            pltpu.SMEM((4, TF), f32),
            pltpu.SMEM((4, TF), f32),
            pltpu.SMEM((TF,), f32),
            pltpu.VMEM((R, Y), jnp.int32),
            pltpu.VMEM((R, Y), f32),
            pltpu.VMEM((3 * R, Y), f32),
            pltpu.VMEM((R + 2 * PAD, Y), f32),
            pltpu.VMEM((R + 2 * PAD, Y), f32),
            pltpu.VMEM((2 * X, Y), f32),
            pltpu.VMEM((16, Y), f32),
            pltpu.VMEM((8, Y), f32),
            pltpu.VMEM((8, Y), f32),
            pltpu.VMEM((88, Y), f32),
            pltpu.VMEM((4, R + 2 * PAD, Y), f32),
            pltpu.VMEM((11, R, Y), f32),
            pltpu.VMEM((2 * X, Y), f32),
            pltpu.VMEM((4, 16, Y), f32),
            pltpu.VMEM((4, 8, Y), f32),
            pltpu.VMEM((4, 64, Y), f32),
            pltpu.VMEM((4, 4, R, Y), f32),
            pltpu.VMEM((3, 1, Y), f32),
            pltpu.VMEM((3, 7, 1, Y), f32),
            pltpu.VMEM((TF, 32, Y), f32),
            pltpu.VMEM((TF, 16, Y), f32),
            pltpu.VMEM((TF, 32, Y), f32),
            pltpu.VMEM((TF * 32, Y), f32),
            pltpu.VMEM((TF * 16, Y), f32),
            pltpu.VMEM((TF * 32, Y), f32),
            pltpu.VMEM((R, Y), f32),
            pltpu.VMEM((TF, 8, Y), f32),
            pltpu.VMEM((TF * 8, Y), f32),
            pltpu.SemaphoreType.DMA((6,)),
            pltpu.SemaphoreType.DMA((12,)),
            pltpu.SemaphoreType.DMA((12,)),
        ],
        compiler_params=pltpu.CompilerParams(
            collective_id=0, has_side_effects=True, vmem_limit_bytes=64000 * 1024
        ),
    )(
        phase_field.reshape(R, Y),
        thermal.reshape(R, Y),
        velocity.reshape(3 * R, Y),
        transfer_slope.T,
        transfer_offset.T,
        transfer_gain,
    )
    return corrected.reshape(3, Z, X, Y), images.reshape(1, 4, X, Y)


def solution(mesh):
    sizes = (mesh.shape["gx"], mesh.shape["gy"], mesh.shape["gz"])
    return jax.shard_map(
        functools.partial(local, sizes),
        mesh=mesh,
        in_specs=(
            P("gz", "gx", "gy"),
            P("gz", "gx", "gy"),
            P(None, "gz", "gx", "gy"),
            P(),
            P(),
            P(),
        ),
        out_specs=(P(None, "gz", "gx", "gy"), P("gz", None, "gx", "gy")),
        check_vma=False,
    )
```

```python
import functools

import jax
import jax.numpy as jnp
from jax import lax
from jax.experimental import pallas as pl
from jax.experimental.pallas import tpu as pltpu
from jax.sharding import PartitionSpec as P

MESH = pl.DeviceIdType.MESH
Z, X, Y = 8, 16, 128
R = Z * X
K = R // 8
TF = 8
PAD = 8
FAR_FIRST = (4, 3, 5, 2, 6, 1, 7)


def lanes(shape):
    return lax.broadcasted_iota(jnp.int32, shape, 1)


def group(v, k):
    return v[8 * k : 8 * k + 8]


def recip(v):
    r = pl.reciprocal(v, approx=True)
    r = r * (2.0 - v * r)
    return r * (2.0 - v * r)


def pack_ends(v):
    lane = lanes((8, Y))
    out = jnp.zeros((8, Y), jnp.float32)
    for k in range(K):
        out = jnp.where(lane // 2 == k, pltpu.roll(group(v, k), 2 * k + 1, 1), out)
    return out


def unpack_ends(below, above):
    lane = lanes((8, Y))
    both = jnp.where(lane % 2 == 0, pltpu.roll(above, Y - 1, 1), pltpu.roll(below, 1, 1))
    return jnp.concatenate([pltpu.roll(both, Y - (2 * k + 1), 1) for k in range(K)], axis=0)


def spread(below, above):
    pieces = []
    for z in range(Z):
        pieces.append(jnp.broadcast_to(below[z : z + 1], (8, Y)))
        pieces.append(jnp.broadcast_to(above[z : z + 1], (8, Y)))
    return jnp.concatenate(pieces, axis=0)


def kernel(
    sizes,
    phase_in,
    thermal_in,
    vel_in,
    slope_in,
    offset_in,
    gain_in,
    corrected,
    images,
    slope,
    offset,
    gain,
    phase_v,
    thermal_v,
    vel_v,
    vel1_pad,
    den_pad,
    s1z,
    s1x,
    s1xu,
    s1y,
    h1,
    v_pad,
    coef,
    edge_z,
    sx,
    sy,
    h,
    grads,
    row_send,
    row_plane,
    row_line,
    send_a,
    send_b,
    send_c,
    recv_a,
    recv_b,
    recv_c,
    vel_sum,
    img_send,
    img_recv,
    in_sem,
    send_sem,
    recv_sem,
    known,
):
    nx, ny, nz = sizes
    ix, iy, iz = lax.axis_index("gx"), lax.axis_index("gy"), lax.axis_index("gz")
    xm, xp = {"gx": lax.rem(ix + nx - 1, nx)}, {"gx": lax.rem(ix + 1, nx)}
    ym, yp = {"gy": lax.rem(iy + ny - 1, ny)}, {"gy": lax.rem(iy + 1, ny)}
    zm, zp = {"gz": lax.rem(iz + nz - 1, nz)}, {"gz": lax.rem(iz + 1, nz)}
    x_first, x_last = ix == 0, ix == nx - 1
    y_first, y_last = iy == 0, iy == ny - 1
    z_first, z_last = iz == 0, iz == nz - 1

    loads = [
        pltpu.make_async_copy(phase_in, phase_v, in_sem.at[0]),
        pltpu.make_async_copy(thermal_in, thermal_v, in_sem.at[1]),
        pltpu.make_async_copy(vel_in, vel_v, in_sem.at[2]),
    ]
    params = [
        pltpu.make_async_copy(slope_in, slope, in_sem.at[3]),
        pltpu.make_async_copy(offset_in, offset, in_sem.at[4]),
        pltpu.make_async_copy(gain_in, gain, in_sem.at[5]),
    ]
    barrier = pltpu.get_barrier_semaphore()
    for device in (zm, zp, ym, yp, xm, xp):
        pl.semaphore_signal(barrier, inc=1, device_id=device, device_id_type=MESH)
    for copy in loads + params:
        copy.start()

    pad = jnp.zeros((PAD, Y), jnp.float32)
    for ref in [den_pad, vel1_pad] + [v_pad.at[j] for j in range(4)]:
        ref[0:PAD] = pad
        ref[PAD + R : PAD + R + PAD] = pad

    def send(src, dst, group_id, device):
        pltpu.make_async_remote_copy(
            src, dst, send_sem.at[group_id], recv_sem.at[group_id], device_id=device, device_id_type=MESH
        ).start()

    def whole(ref, group_id):
        return pltpu.make_async_remote_copy(
            ref, ref, send_sem.at[group_id], recv_sem.at[group_id], device_id=xp, device_id_type=MESH
        )

    def in_plane(dx, dy):
        return {"gx": lax.rem(ix + dx, nx), "gy": lax.rem(iy + dy, ny)}

    def hello(which, dx, dy):
        pl.semaphore_signal(
            known.at[which], inc=1, device_id=in_plane(dx, dy), device_id_type=MESH
        )

    lane = lanes((R, Y))
    row = lax.broadcasted_iota(jnp.int32, (R, Y), 0)
    in_x = row % X

    for copy in loads:
        copy.wait()
    den = (1.0 + 9.0 * phase_v[...].astype(jnp.float32)) * thermal_v[...]
    den_pad[PAD : PAD + R] = den
    vel0, vel1, vel2 = vel_v[0:R], vel_v[R : 2 * R], vel_v[2 * R : 3 * R]
    vel1_pad[PAD : PAD + R] = vel1
    s1z[0:X] = den[0:X]
    s1z[X : 2 * X] = vel0[0:X]
    s1x[0:8] = den_pad[pl.ds(PAD, 8, stride=X)]
    s1x[8:16] = vel1_pad[pl.ds(PAD, 8, stride=X)]
    s1xu[...] = den_pad[pl.ds(PAD + X - 1, 8, stride=X)]
    ends = pack_ends(den)
    lane8 = lanes((8, Y))
    for k in range(K):
        ends = jnp.where(lane8 == 2 * K + k, pltpu.roll(group(vel2, k), 2 * K + k, 1), ends)
    s1y[...] = ends

    pl.semaphore_wait(barrier, 6)

    send(den_pad.at[pl.ds(PAD + R - X, X)], h1.at[pl.ds(0, 16)], 0, zp)
    send(s1z, h1.at[pl.ds(16, 32)], 0, zm)
    send(s1xu, h1.at[pl.ds(48, 8)], 0, xp)
    send(s1x, h1.at[pl.ds(56, 16)], 0, xm)
    send(s1y, h1.at[pl.ds(72, 8)], 0, yp)
    send(s1y, h1.at[pl.ds(80, 8)], 0, ym)
    whole(h1, 0).wait_recv()
    wide = nx == 8 and ny == 8
    if wide:
        for dx, dy in ((2, 0), (6, 0), (0, 2), (0, 6)):
            hello(0, dx, dy)

    def face(first, own, other):
        return jnp.where(first, own, other)

    zb = jnp.concatenate([face(z_first, den[0:X], h1[0:16]), den[: R - X]], axis=0)
    za = jnp.concatenate([den[X:], face(z_last, den[R - X :], h1[16:32])], axis=0)
    bx = spread(h1[48:56], h1[56:64])
    xb = jnp.where(in_x == 0, face(x_first, den, bx), den_pad[PAD - 1 : PAD - 1 + R])
    xa = jnp.where(in_x == X - 1, face(x_last, den, bx), den_pad[PAD + 1 : PAD + 1 + R])
    by = unpack_ends(h1[72:80], h1[80:88])
    yb = jnp.where(lane == 0, face(y_first, den, by), pltpu.roll(den, 1, 1))
    ya = jnp.where(lane == Y - 1, face(y_last, den, by), pltpu.roll(den, Y - 1, 1))
    low_z, up_z = 2.0 * recip(den + zb), 2.0 * recip(den + za)
    low_x, up_x = 2.0 * recip(den + xb), 2.0 * recip(den + xa)
    low_y, up_y = 2.0 * recip(den + yb), 2.0 * recip(den + ya)
    inverse = recip(low_z + up_z + low_x + up_x + low_y + up_y)

    def keep(flag):
        return jnp.where(flag, 0.0, 1.0)

    zero = jnp.zeros((R, Y), jnp.float32)
    coef[0] = low_z
    coef[1] = low_x
    coef[2] = low_y
    coef[3] = up_z
    coef[4] = jnp.where(in_x == X - 1, 0.0, up_x)
    coef[5] = jnp.where(lane == Y - 1, 0.0, up_y)
    coef[6] = jnp.where(in_x == 0, 0.0, low_x)
    coef[7] = jnp.where(lane == 0, 0.0, low_y)
    coef[8] = jnp.where(
        in_x == 0, low_x * keep(x_first), jnp.where(in_x == X - 1, up_x * keep(x_last), zero)
    )
    coef[9] = jnp.where(
        lane == 0, low_y * keep(y_first), jnp.where(lane == Y - 1, up_y * keep(y_last), zero)
    )
    coef[10] = inverse
    edge_z[0:X] = low_z[0:X] * keep(z_first)
    edge_z[X : 2 * X] = up_z[R - X :] * keep(z_last)

    above0 = jnp.concatenate([vel0[X:], h1[32:48] * keep(z_last)], axis=0)
    bv = spread(h1[56:64], h1[64:72])
    above1 = jnp.where(in_x == X - 1, bv * keep(x_last), vel1_pad[PAD + 1 : PAD + 1 + R])
    ends_above = h1[80:88]
    bw = jnp.concatenate(
        [pltpu.roll(ends_above, Y - 1 - (2 * K + k), 1) for k in range(K)], axis=0
    )
    above2 = jnp.where(lane == Y - 1, bw * keep(y_last), pltpu.roll(vel2, Y - 1, 1))
    rhs = -(((above0 - vel0) + (above1 - vel1)) + (above2 - vel2))

    def hand_out(buf, recv, group_id, steps):
        rows = buf.shape[1]
        for k in steps:
            to = lax.rem(iz + k, nz)
            send(buf.at[to], recv.at[pl.ds(iz * rows, rows)], group_id, {"gz": to})

    def scatter(fields, buf, recv, group_id, steps):
        for q, ref in enumerate(fields):
            for t in range(TF):
                for r in range(2):
                    at = 16 * q + 8 * r
                    buf[t, at : at + 8] = ref[pl.ds(r * (R // 2) + t, 8, stride=8)]
        rows = 16 * len(fields)
        hand_out(buf, recv, group_id, steps)
        recv[pl.ds(pl.multiple_of(iz * rows, rows), rows)] = buf[iz]

    folded = []

    def fold(value):
        value = jnp.sum(value.reshape(K, 8, Y), axis=0)
        for step in (64, 32, 16):
            value = value + pltpu.roll(value, step, 1)
        m = len(folded)
        before = folded[-1] if folded else jnp.zeros((8, Y), jnp.float32)
        folded.append(jnp.where(lane8 // 16 == m, value, before))

    def gradient(j, v, z_low, x_low, y_low):
        g0, g1, g2 = coef[0] * v - z_low, coef[1] * v - x_low, coef[2] * v - y_low
        grads[j, 0] = g0
        grads[j, 1] = g1
        grads[j, 2] = g2
        grads[j, 3] = g0 + g1 + g2

    vel_sum[...] = vel0 + vel1 + vel2
    scaled = rhs
    last = None
    for j in range(4):
        v = coef[10] * scaled
        own = v_pad.at[j]
        own[PAD : PAD + R] = v
        sx[j, 8:16] = own[pl.ds(PAD + X - 1, 8, stride=X)]
        sy[j] = pack_ends(v)
        hj = h.at[j]
        send(own.at[pl.ds(PAD + R - X, X)], hj.at[pl.ds(0, 16)], 1 + j, zp)
        if j < 3:
            send(own.at[pl.ds(PAD, X)], hj.at[pl.ds(32, 16)], 1 + j, zm)
        send(sy.at[j], hj.at[pl.ds(24, 8)], 1 + j, yp)
        if j < 3:
            send(sy.at[j], hj.at[pl.ds(56, 8)], 1 + j, ym)
        send(sx.at[j, pl.ds(8, 8)], hj.at[pl.ds(16, 8)], 1 + j, xp)
        if j < 3:
            sx[j, 0:8] = own[pl.ds(PAD, 8, stride=X)]
            send(sx.at[j, pl.ds(0, 8)], hj.at[pl.ds(48, 8)], 1 + j, xm)

        if j:
            fold(last[0] * last[5])
            gradient(j - 1, last[0], *last[2:5])
        fold(scaled * v)
        z_low = coef[0, X:R] * v[: R - X]
        x_low = coef[6] * own[PAD - 1 : PAD - 1 + R]
        y_low = coef[7] * pltpu.roll(v, 1, 1)
        if j < 3:
            z_up = coef[3, 0 : R - X] * v[X:]
            x_up = coef[4] * own[PAD + 1 : PAD + 1 + R]
            y_up = coef[5] * pltpu.roll(v, Y - 1, 1)
            rest = (x_low + x_up) + (y_low + y_up)
        if j == 1:
            scatter([vel_sum, grads.at[0, 3]], send_a, recv_a, 8, FAR_FIRST[1:])
        if j == 2:
            hand_out(send_a, recv_a, 8, FAR_FIRST[:1])
            scatter([grads.at[1, 3]], send_b, recv_b, 9, FAR_FIRST)

        if j < 3:
            if wide and j == 1:
                pl.semaphore_wait(known.at[0], 4)
                hello(1, 4, 0)
                hello(1, 0, 4)
            if wide and j == 2:
                pl.semaphore_wait(known.at[1], 2)
            whole(hj, 1 + j).wait_recv()
            z_low = jnp.concatenate([edge_z[0:X] * hj[0:16], z_low], axis=0)
            z_up = jnp.concatenate([z_up, edge_z[X : 2 * X] * hj[32:48]], axis=0)
            x_edge = coef[8] * spread(hj[16:24], hj[48:56])
            y_edge = coef[9] * unpack_ends(hj[24:32], hj[56:64])
            image = ((z_low + z_up) + rest) + (x_edge + y_edge)
            x_low = x_low + jnp.where(in_x == 0, x_edge, 0.0)
            y_low = y_low + jnp.where(lane == 0, y_edge, 0.0)
            last = (v, None, z_low, x_low, y_low, image)
            scaled = image
        else:
            whole(hj.at[pl.ds(0, 32)], 1 + j).wait_recv()
            z_low = jnp.concatenate([edge_z[0:X] * hj[0:16], z_low], axis=0)
            x_edge = coef[8] * spread(hj[16:24], hj[16:24])
            y_edge = coef[9] * unpack_ends(hj[24:32], hj[24:32])
            x_low = x_low + jnp.where(in_x == 0, x_edge, 0.0)
            y_low = y_low + jnp.where(lane == 0, y_edge, 0.0)
            fold((2.0 * v) * ((z_low + x_low) + y_low))

    line = jnp.sum(folded[-1], axis=0, keepdims=True)
    row_send[0] = line
    others = [(dx, dy) for dx in range(nx) for dy in range(ny) if dx or dy]

    def hops(apart):
        dx, dy = apart
        return min(dx, nx - dx) / 2 + min(dy, ny - dy)

    others.sort(key=hops, reverse=True)
    for at, apart in enumerate(others):
        send(row_send.at[0], row_plane.at[pl.ds(at, 1)], 5, in_plane(*apart))
    row_plane[pl.ds(len(others), 1)] = line
    gradient(3, v, z_low, x_low, y_low)
    scatter([grads.at[2, 3], grads.at[3, 3]], send_c, recv_c, 10, FAR_FIRST)
    whole(row_plane.at[pl.ds(0, len(others))], 5).wait_recv()
    line = jnp.sum(row_plane[0 : len(others) + 1], axis=0, keepdims=True)
    row_send[1] = line
    for k in FAR_FIRST:
        send(row_send.at[1], row_line.at[pl.ds(k - 1, 1)], 6, {"gz": lax.rem(iz + k, nz)})
    row_line[nz - 1 : nz] = line
    for ref, group_id in ((recv_a, 8), (recv_b, 9), (recv_c, 10)):
        whole(ref.at[pl.ds(0, ref.shape[0] // nz * (nz - 1))], group_id).wait_recv()
    for copy in params:
        copy.wait()
    whole(row_line.at[pl.ds(0, nz - 1)], 6).wait_recv()
    line = jnp.sum(row_line[...], axis=0, keepdims=True)
    lane1 = lanes((1, Y))
    m = [jnp.sum(jnp.where(lane1 // 16 == i, line, 0.0), axis=1, keepdims=True) for i in range(8)]

    a = [[m[i + j] - m[i + j + 1] for j in range(4)] for i in range(4)]
    b = [m[i] for i in range(4)]
    pivots = []
    for p in range(4):
        ok = a[p][p] > 1e-7 * (m[2 * p] - m[2 * p + 1])
        pivots.append(jnp.where(ok, 1.0 / jnp.where(ok, a[p][p], 1.0), 0.0))
        for i in range(p + 1, 4):
            factor = a[p][i] * pivots[p]
            for j in range(i, 4):
                a[i][j] = a[i][j] - factor * a[p][j]
            b[i] = b[i] - factor * b[p]
    c = [None] * 4
    for p in reversed(range(4)):
        value = b[p]
        for j in range(p + 1, 4):
            value = value - a[p][j] * c[j]
        c[p] = value * pivots[p]

    field = []
    for z in range(Z):
        halves = []
        for r in range(2):
            at = 2 * z + r
            value = recv_a[pl.ds(at, 8, stride=32)]
            value = value - c[0] * recv_a[pl.ds(16 + at, 8, stride=32)]
            value = value - c[1] * recv_b[pl.ds(at, 8, stride=16)]
            value = value - c[2] * recv_c[pl.ds(at, 8, stride=32)]
            value = value - c[3] * recv_c[pl.ds(16 + at, 8, stride=32)]
            halves.append(value)
        field.append(jnp.concatenate(halves, axis=0))
    sub = lax.broadcasted_iota(jnp.int32, (8, Y), 0)
    for k in FAR_FIRST + (0,):
        t = lax.rem(iz + k, nz)
        half = 0.5 / (Z * nz) * gain[t]
        slopes = [0.5 * slope[i, t] for i in range(4)]
        offsets = [0.5 * offset[i, t] for i in range(4)]
        through = jnp.ones((16, Y), jnp.float32)
        colors = [jnp.zeros((16, Y), jnp.float32) for _ in range(3)]
        for z in range(Z):
            weight = through * (half + half * jnp.tanh(slopes[3] * field[z] + offsets[3]))
            through = through - weight
            for i in range(3):
                colors[i] = colors[i] + weight * jnp.tanh(slopes[i] * field[z] + offsets[i])
        lines = [[None, None] for _ in range(4)]
        for r in range(2):
            here = through[8 * r : 8 * r + 8]
            before = jnp.where(sub >= 1, pltpu.roll(here, 1, 0), 1.0)
            for step in (1, 2, 4):
                before = before * jnp.where(sub >= step, pltpu.roll(before, step, 0), 1.0)
            for i in range(3):
                color = 0.5 * (colors[i][8 * r : 8 * r + 8] + (1.0 - here))
                lines[i][r] = jnp.sum(before * color, axis=0, keepdims=True)
            lines[3][r] = (1.0 - before * here)[7:8]
        tile = jnp.concatenate([lines[i][r] for i in range(4) for r in range(2)], axis=0)
        if k:
            img_send[t] = tile
            send(img_send.at[t], img_recv.at[pl.ds(iz * 8, 8)], 11, {"gz": t})
        else:
            img_recv[pl.ds(pl.multiple_of(iz * 8, 8), 8)] = tile
    for d in range(3):
        value = vel_v[d * R : (d + 1) * R]
        for j in range(4):
            value = value - c[j] * grads[j, d]
        corrected[d * R : (d + 1) * R] = value
    whole(img_recv.at[pl.ds(0, 8 * (nz - 1))], 11).wait_recv()
    for i in range(4):
        for r in range(2):
            images[i * X + 8 * r : i * X + 8 * r + 8] = img_recv[pl.ds(2 * i + r, 8, stride=8)]

    whole(h1, 0).wait_send()
    for j in range(4):
        whole(h.at[j, pl.ds(0, 64 if j < 3 else 32)], 1 + j).wait_send()
    whole(row_plane.at[pl.ds(0, len(others))], 5).wait_send()
    whole(row_line.at[pl.ds(0, nz - 1)], 6).wait_send()
    for ref, group_id in ((recv_a, 8), (recv_b, 9), (recv_c, 10), (img_recv, 11)):
        whole(ref.at[pl.ds(0, ref.shape[0] // nz * (nz - 1))], group_id).wait_send()


def local(sizes, phase_field, thermal, velocity, transfer_slope, transfer_offset, transfer_gain):
    f32 = jnp.float32
    hbm = pl.BlockSpec(memory_space=pltpu.HBM)
    vmem = pl.BlockSpec(memory_space=pltpu.VMEM)
    corrected, images = pl.pallas_call(
        functools.partial(kernel, sizes),
        out_shape=(
            jax.ShapeDtypeStruct((3 * R, Y), f32),
            jax.ShapeDtypeStruct((4 * X, Y), f32),
        ),
        in_specs=[hbm] * 6,
        out_specs=(vmem, vmem),
        scratch_shapes=[
            pltpu.SMEM((4, TF), f32),
            pltpu.SMEM((4, TF), f32),
            pltpu.SMEM((TF,), f32),
            pltpu.VMEM((R, Y), jnp.int32),
            pltpu.VMEM((R, Y), f32),
            pltpu.VMEM((3 * R, Y), f32),
            pltpu.VMEM((R + 2 * PAD, Y), f32),
            pltpu.VMEM((R + 2 * PAD, Y), f32),
            pltpu.VMEM((2 * X, Y), f32),
            pltpu.VMEM((16, Y), f32),
            pltpu.VMEM((8, Y), f32),
            pltpu.VMEM((8, Y), f32),
            pltpu.VMEM((88, Y), f32),
            pltpu.VMEM((4, R + 2 * PAD, Y), f32),
            pltpu.VMEM((11, R, Y), f32),
            pltpu.VMEM((2 * X, Y), f32),
            pltpu.VMEM((4, 16, Y), f32),
            pltpu.VMEM((4, 8, Y), f32),
            pltpu.VMEM((4, 64, Y), f32),
            pltpu.VMEM((4, 4, R, Y), f32),
            pltpu.VMEM((2, 1, Y), f32),
            pltpu.VMEM((sizes[0] * sizes[1], Y), f32),
            pltpu.VMEM((sizes[2], Y), f32),
            pltpu.VMEM((TF, 32, Y), f32),
            pltpu.VMEM((TF, 16, Y), f32),
            pltpu.VMEM((TF, 32, Y), f32),
            pltpu.VMEM((TF * 32, Y), f32),
            pltpu.VMEM((TF * 16, Y), f32),
            pltpu.VMEM((TF * 32, Y), f32),
            pltpu.VMEM((R, Y), f32),
            pltpu.VMEM((TF, 8, Y), f32),
            pltpu.VMEM((TF * 8, Y), f32),
            pltpu.SemaphoreType.DMA((6,)),
            pltpu.SemaphoreType.DMA((12,)),
            pltpu.SemaphoreType.DMA((12,)),
            pltpu.SemaphoreType.REGULAR((2,)),
        ],
        compiler_params=pltpu.CompilerParams(
            collective_id=0, has_side_effects=True, vmem_limit_bytes=16 * 2**20
        ),
    )(
        *(
            pltpu.with_memory_space_constraint(value, pltpu.HBM)
            for value in (
                phase_field.reshape(R, Y),
                thermal.reshape(R, Y),
                velocity.reshape(3 * R, Y),
                transfer_slope.T,
                transfer_offset.T,
                transfer_gain,
            )
        )
    )
    return corrected.reshape(3, Z, X, Y), images.reshape(1, 4, X, Y)


def solution(mesh):
    sizes = (mesh.shape["gx"], mesh.shape["gy"], mesh.shape["gz"])
    return jax.shard_map(
        functools.partial(local, sizes),
        mesh=mesh,
        in_specs=(
            P("gz", "gx", "gy"),
            P("gz", "gx", "gy"),
            P(None, "gz", "gx", "gy"),
            P(),
            P(),
            P(),
        ),
        out_specs=(P(None, "gz", "gx", "gy"), P("gz", None, "gx", "gy")),
        check_vma=False,
    )
```

```python
import functools

import jax
import jax.numpy as jnp
from jax import lax
from jax.experimental import pallas as pl
from jax.experimental.pallas import tpu as pltpu
from jax.sharding import PartitionSpec as P

MESH = pl.DeviceIdType.MESH
Z, X, Y = 8, 16, 128
R = Z * X
K = R // 8
TF = 8
PAD = 8
FAR_FIRST = (4, 3, 5, 2, 6, 1, 7)


def lanes(shape):
    return lax.broadcasted_iota(jnp.int32, shape, 1)


def group(v, k):
    return v[8 * k : 8 * k + 8]


def recip(v):
    r = pl.reciprocal(v, approx=True)
    r = r * (2.0 - v * r)
    return r * (2.0 - v * r)


def pack_ends(v):
    lane = lanes((8, Y))
    out = jnp.zeros((8, Y), jnp.float32)
    for k in range(K):
        out = jnp.where(lane // 2 == k, pltpu.roll(group(v, k), 2 * k + 1, 1), out)
    return out


def merge(below, above):
    even = lanes((8, Y)) % 2 == 0
    return jnp.where(even, pltpu.roll(above, Y - 1, 1), pltpu.roll(below, 1, 1))


def unpack(both):
    return jnp.concatenate([pltpu.roll(both, Y - (2 * k + 1), 1) for k in range(K)], axis=0)


def rows_of(first, second):
    return jnp.concatenate(
        [jnp.broadcast_to(first, (8, Y)), jnp.broadcast_to(second, (8, Y))], axis=0
    )


def spread(below, above):
    pieces = []
    for z in range(Z):
        pieces.append(jnp.broadcast_to(below[z : z + 1], (8, Y)))
        pieces.append(jnp.broadcast_to(above[z : z + 1], (8, Y)))
    return jnp.concatenate(pieces, axis=0)


def kernel(
    sizes,
    phase_in,
    thermal_in,
    vel_in,
    slope_in,
    offset_in,
    gain_in,
    corrected,
    images,
    slope,
    offset,
    gain,
    phase_v,
    thermal_v,
    vel_v,
    vel1_pad,
    den_pad,
    s1z,
    s1x,
    s1xu,
    s1y,
    h1,
    v_pad,
    coef,
    edge_z,
    weights,
    stat_z,
    stat_x,
    stat_y,
    stat,
    stat_m,
    scaled_v,
    dz,
    dx,
    dy,
    h,
    grads,
    row_send,
    row_plane,
    row_line,
    send_a,
    send_c,
    recv_a,
    recv_c,
    vel_sum,
    img_send,
    img_recv,
    in_sem,
    send_sem,
    recv_sem,
    known,
):
    nx, ny, nz = sizes
    ix, iy, iz = lax.axis_index("gx"), lax.axis_index("gy"), lax.axis_index("gz")
    xm, xp = {"gx": lax.rem(ix + nx - 1, nx)}, {"gx": lax.rem(ix + 1, nx)}
    ym, yp = {"gy": lax.rem(iy + ny - 1, ny)}, {"gy": lax.rem(iy + 1, ny)}
    zm, zp = {"gz": lax.rem(iz + nz - 1, nz)}, {"gz": lax.rem(iz + 1, nz)}
    x_first, x_last = ix == 0, ix == nx - 1
    y_first, y_last = iy == 0, iy == ny - 1
    z_first, z_last = iz == 0, iz == nz - 1

    loads = [
        pltpu.make_async_copy(phase_in, phase_v, in_sem.at[0]),
        pltpu.make_async_copy(thermal_in, thermal_v, in_sem.at[1]),
        pltpu.make_async_copy(vel_in, vel_v, in_sem.at[2]),
    ]
    params = [
        pltpu.make_async_copy(slope_in, slope, in_sem.at[3]),
        pltpu.make_async_copy(offset_in, offset, in_sem.at[4]),
        pltpu.make_async_copy(gain_in, gain, in_sem.at[5]),
    ]
    barrier = pltpu.get_barrier_semaphore()
    for device in (zm, zp, ym, yp, xm, xp):
        pl.semaphore_signal(barrier, inc=1, device_id=device, device_id_type=MESH)
    for copy in loads + params:
        copy.start()

    pad = jnp.zeros((PAD, Y), jnp.float32)
    for ref in [den_pad, vel1_pad] + [v_pad.at[j] for j in range(4)]:
        ref[0:PAD] = pad
        ref[PAD + R : PAD + R + PAD] = pad

    def send(src, dst, group_id, device):
        pltpu.make_async_remote_copy(
            src, dst, send_sem.at[group_id], recv_sem.at[group_id], device_id=device, device_id_type=MESH
        ).start()

    def whole(ref, group_id):
        return pltpu.make_async_remote_copy(
            ref, ref, send_sem.at[group_id], recv_sem.at[group_id], device_id=xp, device_id_type=MESH
        )

    def in_plane(dx, dy):
        return {"gx": lax.rem(ix + dx, nx), "gy": lax.rem(iy + dy, ny)}

    def hello(which, dx, dy):
        pl.semaphore_signal(
            known.at[which], inc=1, device_id=in_plane(dx, dy), device_id_type=MESH
        )

    lane = lanes((R, Y))
    row = lax.broadcasted_iota(jnp.int32, (R, Y), 0)
    in_x = row % X

    for copy in loads:
        copy.wait()
    den = (1.0 + 9.0 * phase_v[...].astype(jnp.float32)) * thermal_v[...]
    den_pad[PAD : PAD + R] = den
    vel0, vel1, vel2 = vel_v[0:R], vel_v[R : 2 * R], vel_v[2 * R : 3 * R]
    vel1_pad[PAD : PAD + R] = vel1
    s1z[0:X] = den[0:X]
    s1z[X : 2 * X] = vel0[0:X]
    s1x[0:8] = den_pad[pl.ds(PAD, 8, stride=X)]
    s1x[8:16] = vel1_pad[pl.ds(PAD, 8, stride=X)]
    s1xu[...] = den_pad[pl.ds(PAD + X - 1, 8, stride=X)]
    ends = pack_ends(den)
    lane8 = lanes((8, Y))
    for k in range(K):
        ends = jnp.where(lane8 == 2 * K + k, pltpu.roll(group(vel2, k), 2 * K + k, 1), ends)
    s1y[...] = ends

    pl.semaphore_wait(barrier, 6)

    send(den_pad.at[pl.ds(PAD + R - X, X)], h1.at[pl.ds(0, 16)], 0, zp)
    send(s1z, h1.at[pl.ds(16, 32)], 0, zm)
    send(s1xu, h1.at[pl.ds(48, 8)], 0, xp)
    send(s1x, h1.at[pl.ds(56, 16)], 0, xm)
    send(s1y, h1.at[pl.ds(72, 8)], 0, yp)
    send(s1y, h1.at[pl.ds(80, 8)], 0, ym)
    whole(h1, 0).wait_recv()
    wide = nx == 8 and ny == 8
    if wide:
        for far in ((2, 0), (6, 0), (0, 2), (0, 6)):
            hello(0, *far)
    for step in (2, 6):
        pl.semaphore_signal(
            known.at[2], inc=1, device_id={"gz": lax.rem(iz + step, nz)}, device_id_type=MESH
        )

    def face(first, own, other):
        return jnp.where(first, own, other)

    zb = jnp.concatenate([face(z_first, den[0:X], h1[0:16]), den[: R - X]], axis=0)
    za = jnp.concatenate([den[X:], face(z_last, den[R - X :], h1[16:32])], axis=0)
    bx = spread(h1[48:56], h1[56:64])
    xb = jnp.where(in_x == 0, face(x_first, den, bx), den_pad[PAD - 1 : PAD - 1 + R])
    xa = jnp.where(in_x == X - 1, face(x_last, den, bx), den_pad[PAD + 1 : PAD + 1 + R])
    by = unpack(merge(h1[72:80], h1[80:88]))
    yb = jnp.where(lane == 0, face(y_first, den, by), pltpu.roll(den, 1, 1))
    ya = jnp.where(lane == Y - 1, face(y_last, den, by), pltpu.roll(den, Y - 1, 1))
    low_z, up_z = 2.0 * recip(den + zb), 2.0 * recip(den + za)
    low_x, up_x = 2.0 * recip(den + xb), 2.0 * recip(den + xa)
    low_y, up_y = 2.0 * recip(den + yb), 2.0 * recip(den + ya)
    inverse = recip(low_z + up_z + low_x + up_x + low_y + up_y)

    def keep(flag):
        return jnp.where(flag, 0.0, 1.0)

    zero = jnp.zeros((R, Y), jnp.float32)
    coef[0] = low_z
    coef[1] = low_x
    coef[2] = low_y
    coef[3] = up_z
    coef[4] = jnp.where(in_x == X - 1, 0.0, up_x)
    coef[5] = jnp.where(lane == Y - 1, 0.0, up_y)
    coef[6] = jnp.where(in_x == 0, 0.0, low_x)
    coef[7] = jnp.where(lane == 0, 0.0, low_y)
    coef[8] = jnp.where(
        in_x == 0, low_x * keep(x_first), jnp.where(in_x == X - 1, up_x * keep(x_last), zero)
    )
    coef[9] = jnp.where(
        lane == 0, low_y * keep(y_first), jnp.where(lane == Y - 1, up_y * keep(y_last), zero)
    )
    coef[10] = inverse
    edge_z[0:X] = low_z[0:X] * keep(z_first)
    edge_z[X : 2 * X] = up_z[R - X :] * keep(z_last)

    weights[0] = inverse * coef[8]
    weights[1] = inverse * coef[9]
    weights[2] = zero
    weights[2, 0:X] = inverse[0:X] * edge_z[0:X]
    weights[2, R - X : R] = inverse[R - X :] * edge_z[X : 2 * X]
    for i in range(3):
        stat_z[0, 16 * i : 16 * i + 16] = weights[i, 0:X]
        stat_z[1, 16 * i : 16 * i + 16] = weights[i, R - X : R]
        face_x = weights.at[i]
        stat_x[0, 8 * i : 8 * i + 8] = face_x[pl.ds(0, 8, stride=X)]
        stat_x[1, 8 * i : 8 * i + 8] = face_x[pl.ds(X - 1, 8, stride=X)]
        stat_y[8 * i : 8 * i + 8] = pack_ends(weights[i])
    send(stat_z.at[1], stat.at[pl.ds(0, 48)], 3, zp)
    send(stat_z.at[0], stat.at[pl.ds(48, 48)], 3, zm)
    send(stat_y, stat.at[pl.ds(96, 24)], 3, yp)
    send(stat_y, stat.at[pl.ds(120, 24)], 3, ym)
    send(stat_x.at[1], stat.at[pl.ds(144, 24)], 3, xp)
    send(stat_x.at[0], stat.at[pl.ds(168, 24)], 3, xm)

    above0 = jnp.concatenate([vel0[X:], h1[32:48] * keep(z_last)], axis=0)
    bv = spread(h1[56:64], h1[64:72])
    above1 = jnp.where(in_x == X - 1, bv * keep(x_last), vel1_pad[PAD + 1 : PAD + 1 + R])
    ends_above = h1[80:88]
    bw = jnp.concatenate(
        [pltpu.roll(ends_above, Y - 1 - (2 * K + k), 1) for k in range(K)], axis=0
    )
    above2 = jnp.where(lane == Y - 1, bw * keep(y_last), pltpu.roll(vel2, Y - 1, 1))
    rhs = -(((above0 - vel0) + (above1 - vel1)) + (above2 - vel2))

    def hand_out(buf, recv, group_id, steps):
        rows = buf.shape[1]
        for k in steps:
            to = lax.rem(iz + k, nz)
            send(buf.at[to], recv.at[pl.ds(iz * rows, rows)], group_id, {"gz": to})

    def scatter(fields, buf, recv, group_id, steps):
        for q, ref in enumerate(fields):
            for t in range(TF):
                for r in range(2):
                    at = 16 * q + 8 * r
                    buf[t, at : at + 8] = ref[pl.ds(r * (R // 2) + t, 8, stride=8)]
        rows = 16 * len(fields)
        hand_out(buf, recv, group_id, steps)
        recv[pl.ds(pl.multiple_of(iz * rows, rows), rows)] = buf[iz]

    folded = []

    def fold(value):
        value = jnp.sum(value.reshape(K, 8, Y), axis=0)
        for step in (64, 32, 16):
            value = value + pltpu.roll(value, step, 1)
        m = len(folded)
        before = folded[-1] if folded else jnp.zeros((8, Y), jnp.float32)
        folded.append(jnp.where(lane8 // 16 == m, value, before))

    def gradient(j, v, z_low, x_low, y_low):
        g0, g1, g2 = coef[0] * v - z_low, coef[1] * v - x_low, coef[2] * v - y_low
        grads[j, 0] = g0
        grads[j, 1] = g1
        grads[j, 2] = g2
        grads[j, 3] = g0 + g1 + g2

    def near(axis, here, count, step):
        return {axis: lax.rem(here + count - step, count)}

    def exchange(p, own, v, inner):
        nxt = coef[10] * inner
        scaled_v[p] = nxt
        hp = h.at[p]
        for side, at in ((1, R - X), (0, 0)):
            dz[p, side, 0:16] = v[at : at + X]
            dz[p, side, 16:32] = nxt[at : at + X]
        q = pack_ends(v)
        dy[p, 0:8] = q
        dy[p, 8:16] = pack_ends(nxt)
        for side, at in ((1, X - 1), (0, 0)):
            dx[p, side, 0:8] = scaled_v.at[p][pl.ds(at, 8, stride=X)]
            dx[p, side, 8:16] = own[pl.ds(PAD + at, 8, stride=X)]
            dx[p, side, 16:24] = q
        signs = ((-1, -1), (-1, 1), (1, -1), (1, 1))
        for i, (a, b) in enumerate(signs):
            row_at = PAD + (R - X if a < 0 else 0) + (X - 1 if b < 0 else 0)
            to = near("gz", iz, nz, a) | near("gx", ix, nx, b)
            send(own.at[pl.ds(row_at, 1)], hp.at[pl.ds(224 + i, 1)], 1 + p, to)
        for i, (a, b) in enumerate(signs):
            to = near("gz", iz, nz, a) | near("gy", iy, ny, b)
            send(dy.at[p, pl.ds(0, 8)], hp.at[pl.ds(128 + 8 * i, 8)], 1 + p, to)
        for i, (a, b) in enumerate(signs):
            to = near("gx", ix, nx, a) | near("gy", iy, ny, b)
            side = 1 if a < 0 else 0
            send(dx.at[p, side, pl.ds(8, 16)], hp.at[pl.ds(160 + 16 * i, 16)], 1 + p, to)
        send(dz.at[p, 1], hp.at[pl.ds(0, 32)], 1 + p, zp)
        send(dz.at[p, 0], hp.at[pl.ds(32, 32)], 1 + p, zm)
        send(dy.at[p], hp.at[pl.ds(96, 16)], 1 + p, yp)
        send(dy.at[p], hp.at[pl.ds(112, 16)], 1 + p, ym)
        send(dx.at[p, 1, pl.ds(0, 16)], hp.at[pl.ds(64, 16)], 1 + p, xp)
        send(dx.at[p, 0, pl.ds(0, 16)], hp.at[pl.ds(80, 16)], 1 + p, xm)

    sub8 = lax.broadcasted_iota(jnp.int32, (8, Y), 0)

    def received(p):
        hp = h.at[p]
        z_faces = (hp[0:16], hp[32:48])
        x_faces = (hp[72:80], hp[88:96])
        return z_faces, x_faces, merge(hp[96:104], hp[112:120])

    def computed(p, v):
        hp = h.at[p]
        corner = [[hp[224 + 2 * a + b : 225 + 2 * a + b] for b in range(2)] for a in range(2)]
        zy = [merge(hp[128 + 16 * a : 136 + 16 * a], hp[136 + 16 * a : 144 + 16 * a]) for a in (0, 1)]
        xy_rows = [[hp[160 + 32 * a + 16 * b : 168 + 32 * a + 16 * b] for b in (0, 1)] for a in (0, 1)]
        xy = [merge(hp[168 + 32 * a : 176 + 32 * a], hp[184 + 32 * a : 192 + 32 * a]) for a in (0, 1)]
        z_faces, x_faces = [], []
        for a, (at, first) in enumerate(((0, 2 * K - 4), (R - X, 0))):
            from_y = jnp.concatenate(
                [pltpu.roll(zy[a], Y - first - 1, 1), pltpu.roll(zy[a], Y - first - 3, 1)], axis=0
            )
            value = hp[16 + 32 * a : 32 + 32 * a]
            value = value + stat[48 * a + 32 : 48 * a + 48] * v[at : at + X]
            value = value + stat[48 * a : 48 * a + 16] * rows_of(corner[a][0], corner[a][1])
            z_faces.append(value + stat[48 * a + 16 : 48 * a + 32] * from_y)
        for a in range(2):
            mine = dx[p, a, 8:16]
            from_z = jnp.where(
                sub8 == 0,
                jnp.broadcast_to(corner[0][a], (8, Y)),
                jnp.broadcast_to(corner[1][a], (8, Y)),
            )
            from_y = jnp.where(
                lane8 == 0, pltpu.roll(xy_rows[a][0], 1, 1), pltpu.roll(xy_rows[a][1], Y - 1, 1)
            )
            at = 144 + 24 * a
            value = hp[64 + 16 * a : 72 + 16 * a] + stat[at : at + 8] * mine
            value = value + stat[at + 8 : at + 16] * from_y
            x_faces.append(value + stat[at + 16 : at + 24] * from_z)
        last_z = 2 * K - 4
        from_z = jnp.where(lane8 < 4, pltpu.roll(zy[0], Y - last_z, 1), pltpu.roll(zy[1], last_z, 1))
        from_x = jnp.where(
            sub8 == 0,
            pltpu.roll(pltpu.roll(xy[0], Y - 2, 1), 1, 0),
            pltpu.roll(pltpu.roll(xy[1], 2, 1), 7, 0),
        )
        both = merge(hp[104:112], hp[120:128])
        both = both + stat_m[8:16] * dy[p, 0:8]
        both = both + stat_m[0:8] * from_x
        return z_faces, x_faces, both + stat_m[16:24] * from_z

    vel_sum[...] = vel0 + vel1 + vel2
    scaled = rhs
    late = None
    for j in range(4):
        p = j // 2
        v = coef[10] * scaled
        own = v_pad.at[j]
        own[PAD : PAD + R] = v
        z_low = coef[0, X:R] * v[: R - X]
        x_low = coef[6] * own[PAD - 1 : PAD - 1 + R]
        y_low = coef[7] * pltpu.roll(v, 1, 1)
        if j < 3:
            z_up = coef[3, 0 : R - X] * v[X:]
            x_up = coef[4] * own[PAD + 1 : PAD + 1 + R]
            y_up = coef[5] * pltpu.roll(v, Y - 1, 1)
            rest = (x_low + x_up) + (y_low + y_up)
        if j % 2 == 0:
            edge = jnp.zeros((X, Y), jnp.float32)
            inner = jnp.concatenate([edge, z_low], axis=0) + jnp.concatenate([z_up, edge], axis=0)
            exchange(p, own, v, inner + rest)
            earlier = late
            if j:
                fold(last[0] * last[4])
                gradient(*earlier)
                gradient(1, *last[:4])
                scatter([vel_sum, grads.at[0, 3], grads.at[1, 3]], send_a, recv_a, 8, FAR_FIRST)
            fold(scaled * v)
            if j == 0:
                if wide:
                    pl.semaphore_wait(known.at[0], 4)
                pl.semaphore_wait(known.at[2], 2)
                whole(stat, 3).wait_recv()
                for i in range(3):
                    stat_m[8 * i : 8 * i + 8] = merge(
                        stat[96 + 8 * i : 104 + 8 * i], stat[120 + 8 * i : 128 + 8 * i]
                    )
            elif wide:
                pl.semaphore_wait(known.at[1], 2)
            whole(h.at[p, pl.ds(0, 228)], 1 + p).wait_recv()
            if wide and j == 0:
                hello(1, 4, 0)
                hello(1, 0, 4)
            z_faces, x_faces, both = received(p)
        else:
            fold(scaled * v)
            z_faces, x_faces, both = following
        z_low = jnp.concatenate([edge_z[0:X] * z_faces[0], z_low], axis=0)
        x_edge = coef[8] * spread(*x_faces)
        y_edge = coef[9] * unpack(both)
        x_low = x_low + jnp.where(in_x == 0, x_edge, 0.0)
        y_low = y_low + jnp.where(lane == 0, y_edge, 0.0)
        if j < 3:
            z_up = jnp.concatenate([z_up, edge_z[X : 2 * X] * z_faces[1]], axis=0)
            scaled = ((z_low + z_up) + rest) + (x_edge + y_edge)
        if j % 2 == 0:
            following = computed(p, v)
            fold(v * scaled)
            late = (j, v, z_low, x_low, y_low)
        elif j == 1:
            last = (v, z_low, x_low, y_low, scaled)
        else:
            fold((2.0 * v) * ((z_low + x_low) + y_low))

    line = jnp.sum(folded[-1], axis=0, keepdims=True)
    row_send[0] = line
    others = [(dx, dy) for dx in range(nx) for dy in range(ny) if dx or dy]

    def hops(apart):
        dx, dy = apart
        return min(dx, nx - dx) / 2 + min(dy, ny - dy)

    others.sort(key=hops, reverse=True)
    for at, apart in enumerate(others):
        send(row_send.at[0], row_plane.at[pl.ds(at, 1)], 5, in_plane(*apart))
    row_plane[pl.ds(len(others), 1)] = line
    gradient(*late)
    gradient(3, v, z_low, x_low, y_low)
    scatter([grads.at[2, 3], grads.at[3, 3]], send_c, recv_c, 10, FAR_FIRST)
    whole(row_plane.at[pl.ds(0, len(others))], 5).wait_recv()
    line = jnp.sum(row_plane[0 : len(others) + 1], axis=0, keepdims=True)
    row_send[1] = line
    for k in FAR_FIRST:
        send(row_send.at[1], row_line.at[pl.ds(k - 1, 1)], 6, {"gz": lax.rem(iz + k, nz)})
    row_line[nz - 1 : nz] = line
    for ref, group_id in ((recv_a, 8), (recv_c, 10)):
        whole(ref.at[pl.ds(0, ref.shape[0] // nz * (nz - 1))], group_id).wait_recv()
    for copy in params:
        copy.wait()
    whole(row_line.at[pl.ds(0, nz - 1)], 6).wait_recv()
    line = jnp.sum(row_line[...], axis=0, keepdims=True)
    lane1 = lanes((1, Y))
    m = [jnp.sum(jnp.where(lane1 // 16 == i, line, 0.0), axis=1, keepdims=True) for i in range(8)]

    a = [[m[i + j] - m[i + j + 1] for j in range(4)] for i in range(4)]
    b = [m[i] for i in range(4)]
    pivots = []
    for p in range(4):
        ok = a[p][p] > 1e-7 * (m[2 * p] - m[2 * p + 1])
        pivots.append(jnp.where(ok, 1.0 / jnp.where(ok, a[p][p], 1.0), 0.0))
        for i in range(p + 1, 4):
            factor = a[p][i] * pivots[p]
            for j in range(i, 4):
                a[i][j] = a[i][j] - factor * a[p][j]
            b[i] = b[i] - factor * b[p]
    c = [None] * 4
    for p in reversed(range(4)):
        value = b[p]
        for j in range(p + 1, 4):
            value = value - a[p][j] * c[j]
        c[p] = value * pivots[p]

    field = []
    for z in range(Z):
        halves = []
        for r in range(2):
            at = 2 * z + r
            value = recv_a[pl.ds(at, 8, stride=48)]
            value = value - c[0] * recv_a[pl.ds(16 + at, 8, stride=48)]
            value = value - c[1] * recv_a[pl.ds(32 + at, 8, stride=48)]
            value = value - c[2] * recv_c[pl.ds(at, 8, stride=32)]
            value = value - c[3] * recv_c[pl.ds(16 + at, 8, stride=32)]
            halves.append(value)
        field.append(jnp.concatenate(halves, axis=0))
    sub = lax.broadcasted_iota(jnp.int32, (8, Y), 0)
    for k in FAR_FIRST + (0,):
        t = lax.rem(iz + k, nz)
        half = 0.5 / (Z * nz) * gain[t]
        slopes = [0.5 * slope[i, t] for i in range(4)]
        offsets = [0.5 * offset[i, t] for i in range(4)]
        through = jnp.ones((16, Y), jnp.float32)
        colors = [jnp.zeros((16, Y), jnp.float32) for _ in range(3)]
        for z in range(Z):
            weight = through * (half + half * jnp.tanh(slopes[3] * field[z] + offsets[3]))
            through = through - weight
            for i in range(3):
                colors[i] = colors[i] + weight * jnp.tanh(slopes[i] * field[z] + offsets[i])
        lines = [[None, None] for _ in range(4)]
        for r in range(2):
            here = through[8 * r : 8 * r + 8]
            before = jnp.where(sub >= 1, pltpu.roll(here, 1, 0), 1.0)
            for step in (1, 2, 4):
                before = before * jnp.where(sub >= step, pltpu.roll(before, step, 0), 1.0)
            for i in range(3):
                color = 0.5 * (colors[i][8 * r : 8 * r + 8] + (1.0 - here))
                lines[i][r] = jnp.sum(before * color, axis=0, keepdims=True)
            lines[3][r] = (1.0 - before * here)[7:8]
        tile = jnp.concatenate([lines[i][r] for i in range(4) for r in range(2)], axis=0)
        if k:
            img_send[t] = tile
            send(img_send.at[t], img_recv.at[pl.ds(iz * 8, 8)], 11, {"gz": t})
        else:
            img_recv[pl.ds(pl.multiple_of(iz * 8, 8), 8)] = tile
    for d in range(3):
        value = vel_v[d * R : (d + 1) * R]
        for j in range(4):
            value = value - c[j] * grads[j, d]
        corrected[d * R : (d + 1) * R] = value
    whole(img_recv.at[pl.ds(0, 8 * (nz - 1))], 11).wait_recv()
    for i in range(4):
        for r in range(2):
            images[i * X + 8 * r : i * X + 8 * r + 8] = img_recv[pl.ds(2 * i + r, 8, stride=8)]

    whole(h1, 0).wait_send()
    whole(stat, 3).wait_send()
    for p in range(2):
        whole(h.at[p, pl.ds(0, 228)], 1 + p).wait_send()
    whole(row_plane.at[pl.ds(0, len(others))], 5).wait_send()
    whole(row_line.at[pl.ds(0, nz - 1)], 6).wait_send()
    for ref, group_id in ((recv_a, 8), (recv_c, 10), (img_recv, 11)):
        whole(ref.at[pl.ds(0, ref.shape[0] // nz * (nz - 1))], group_id).wait_send()


def local(sizes, phase_field, thermal, velocity, transfer_slope, transfer_offset, transfer_gain):
    f32 = jnp.float32
    hbm = pl.BlockSpec(memory_space=pltpu.HBM)
    vmem = pl.BlockSpec(memory_space=pltpu.VMEM)
    corrected, images = pl.pallas_call(
        functools.partial(kernel, sizes),
        out_shape=(
            jax.ShapeDtypeStruct((3 * R, Y), f32),
            jax.ShapeDtypeStruct((4 * X, Y), f32),
        ),
        in_specs=[hbm] * 6,
        out_specs=(vmem, vmem),
        scratch_shapes=[
            pltpu.SMEM((4, TF), f32),
            pltpu.SMEM((4, TF), f32),
            pltpu.SMEM((TF,), f32),
            pltpu.VMEM((R, Y), jnp.int32),
            pltpu.VMEM((R, Y), f32),
            pltpu.VMEM((3 * R, Y), f32),
            pltpu.VMEM((R + 2 * PAD, Y), f32),
            pltpu.VMEM((R + 2 * PAD, Y), f32),
            pltpu.VMEM((2 * X, Y), f32),
            pltpu.VMEM((16, Y), f32),
            pltpu.VMEM((8, Y), f32),
            pltpu.VMEM((8, Y), f32),
            pltpu.VMEM((88, Y), f32),
            pltpu.VMEM((4, R + 2 * PAD, Y), f32),
            pltpu.VMEM((11, R, Y), f32),
            pltpu.VMEM((2 * X, Y), f32),
            pltpu.VMEM((3, R, Y), f32),
            pltpu.VMEM((2, 48, Y), f32),
            pltpu.VMEM((2, 24, Y), f32),
            pltpu.VMEM((24, Y), f32),
            pltpu.VMEM((192, Y), f32),
            pltpu.VMEM((24, Y), f32),
            pltpu.VMEM((2, R, Y), f32),
            pltpu.VMEM((2, 2, 32, Y), f32),
            pltpu.VMEM((2, 2, 24, Y), f32),
            pltpu.VMEM((2, 16, Y), f32),
            pltpu.VMEM((2, 232, Y), f32),
            pltpu.VMEM((4, 4, R, Y), f32),
            pltpu.VMEM((2, 1, Y), f32),
            pltpu.VMEM((sizes[0] * sizes[1], Y), f32),
            pltpu.VMEM((sizes[2], Y), f32),
            pltpu.VMEM((TF, 48, Y), f32),
            pltpu.VMEM((TF, 32, Y), f32),
            pltpu.VMEM((TF * 48, Y), f32),
            pltpu.VMEM((TF * 32, Y), f32),
            pltpu.VMEM((R, Y), f32),
            pltpu.VMEM((TF, 8, Y), f32),
            pltpu.VMEM((TF * 8, Y), f32),
            pltpu.SemaphoreType.DMA((6,)),
            pltpu.SemaphoreType.DMA((12,)),
            pltpu.SemaphoreType.DMA((12,)),
            pltpu.SemaphoreType.REGULAR((3,)),
        ],
        compiler_params=pltpu.CompilerParams(
            collective_id=0, has_side_effects=True, vmem_limit_bytes=16 * 2**20
        ),
    )(
        *(
            pltpu.with_memory_space_constraint(value, pltpu.HBM)
            for value in (
                phase_field.reshape(R, Y),
                thermal.reshape(R, Y),
                velocity.reshape(3 * R, Y),
                transfer_slope.T,
                transfer_offset.T,
                transfer_gain,
            )
        )
    )
    return corrected.reshape(3, Z, X, Y), images.reshape(1, 4, X, Y)


def solution(mesh):
    sizes = (mesh.shape["gx"], mesh.shape["gy"], mesh.shape["gz"])
    return jax.shard_map(
        functools.partial(local, sizes),
        mesh=mesh,
        in_specs=(
            P("gz", "gx", "gy"),
            P("gz", "gx", "gy"),
            P(None, "gz", "gx", "gy"),
            P(),
            P(),
            P(),
        ),
        out_specs=(P(None, "gz", "gx", "gy"), P("gz", None, "gx", "gy")),
        check_vma=False,
    )
```

```python
import functools

import jax
import jax.numpy as jnp
from jax import lax
from jax.experimental import pallas as pl
from jax.experimental.pallas import tpu as pltpu
from jax.sharding import PartitionSpec as P

MESH = pl.DeviceIdType.MESH
Z, X, Y = 8, 16, 128
R = Z * X
K = R // 8
TF = 8
PAD = 8
FAR_FIRST = (4, 3, 5, 2, 6, 1, 7)


def lanes(shape):
    return lax.broadcasted_iota(jnp.int32, shape, 1)


def group(v, k):
    return v[8 * k : 8 * k + 8]


def recip(v):
    r = pl.reciprocal(v, approx=True)
    r = r * (2.0 - v * r)
    return r * (2.0 - v * r)


def pack_ends(v):
    lane = lanes((8, Y))
    out = jnp.zeros((8, Y), jnp.float32)
    for k in range(K):
        out = jnp.where(lane // 2 == k, pltpu.roll(group(v, k), 2 * k + 1, 1), out)
    return out


def merge(below, above):
    even = lanes((8, Y)) % 2 == 0
    return jnp.where(even, pltpu.roll(above, Y - 1, 1), pltpu.roll(below, 1, 1))


def unpack(both):
    return jnp.concatenate([pltpu.roll(both, Y - (2 * k + 1), 1) for k in range(K)], axis=0)


def rows_of(first, second):
    return jnp.concatenate(
        [jnp.broadcast_to(first, (8, Y)), jnp.broadcast_to(second, (8, Y))], axis=0
    )


def spread(below, above):
    pieces = []
    for z in range(Z):
        pieces.append(jnp.broadcast_to(below[z : z + 1], (8, Y)))
        pieces.append(jnp.broadcast_to(above[z : z + 1], (8, Y)))
    return jnp.concatenate(pieces, axis=0)


def kernel(
    sizes,
    phase_in,
    thermal_in,
    vel_in,
    slope_in,
    offset_in,
    gain_in,
    corrected,
    images,
    slope,
    offset,
    gain,
    phase_v,
    thermal_v,
    vel_v,
    vel1_pad,
    den_pad,
    s1z,
    s1x,
    s1xu,
    s1y,
    h1,
    v_pad,
    coef,
    edge_z,
    weights,
    stat_z,
    stat_x,
    stat_y,
    stat,
    stat_m,
    scaled_v,
    dz,
    dx,
    dy,
    h,
    grads,
    row_send,
    row_plane,
    row_line,
    send_a,
    send_c,
    recv_a,
    recv_c,
    vel_sum,
    img_send,
    img_recv,
    in_sem,
    send_sem,
    recv_sem,
    known,
):
    nx, ny, nz = sizes
    ix, iy, iz = lax.axis_index("gx"), lax.axis_index("gy"), lax.axis_index("gz")
    xm, xp = {"gx": lax.rem(ix + nx - 1, nx)}, {"gx": lax.rem(ix + 1, nx)}
    ym, yp = {"gy": lax.rem(iy + ny - 1, ny)}, {"gy": lax.rem(iy + 1, ny)}
    zm, zp = {"gz": lax.rem(iz + nz - 1, nz)}, {"gz": lax.rem(iz + 1, nz)}
    x_first, x_last = ix == 0, ix == nx - 1
    y_first, y_last = iy == 0, iy == ny - 1
    z_first, z_last = iz == 0, iz == nz - 1

    loads = [
        pltpu.make_async_copy(phase_in, phase_v, in_sem.at[0]),
        pltpu.make_async_copy(thermal_in, thermal_v, in_sem.at[1]),
        pltpu.make_async_copy(vel_in, vel_v, in_sem.at[2]),
    ]
    params = [
        pltpu.make_async_copy(slope_in, slope, in_sem.at[3]),
        pltpu.make_async_copy(offset_in, offset, in_sem.at[4]),
        pltpu.make_async_copy(gain_in, gain, in_sem.at[5]),
    ]
    for copy in loads:
        copy.start()
    barrier = pltpu.get_barrier_semaphore()
    for device in (zm, zp, ym, yp, xm, xp):
        pl.semaphore_signal(barrier, inc=1, device_id=device, device_id_type=MESH)
    for copy in params:
        copy.start()

    pad = jnp.zeros((PAD, Y), jnp.float32)
    for ref in [den_pad, vel1_pad] + [v_pad.at[j] for j in range(4)]:
        ref[0:PAD] = pad
        ref[PAD + R : PAD + R + PAD] = pad

    def send(src, dst, group_id, device):
        pltpu.make_async_remote_copy(
            src, dst, send_sem.at[group_id], recv_sem.at[group_id], device_id=device, device_id_type=MESH
        ).start()

    def whole(ref, group_id):
        return pltpu.make_async_remote_copy(
            ref, ref, send_sem.at[group_id], recv_sem.at[group_id], device_id=xp, device_id_type=MESH
        )

    def in_plane(dx, dy):
        return {"gx": lax.rem(ix + dx, nx), "gy": lax.rem(iy + dy, ny)}

    def hello(which, dx, dy):
        pl.semaphore_signal(
            known.at[which], inc=1, device_id=in_plane(dx, dy), device_id_type=MESH
        )

    lane = lanes((R, Y))
    row = lax.broadcasted_iota(jnp.int32, (R, Y), 0)
    in_x = row % X

    for copy in loads:
        copy.wait()
    den = (1.0 + 9.0 * phase_v[...].astype(jnp.float32)) * thermal_v[...]
    den_pad[PAD : PAD + R] = den
    vel0, vel1, vel2 = vel_v[0:R], vel_v[R : 2 * R], vel_v[2 * R : 3 * R]
    vel1_pad[PAD : PAD + R] = vel1
    s1z[0:X] = den[0:X]
    s1z[X : 2 * X] = vel0[0:X]
    s1x[0:8] = den_pad[pl.ds(PAD, 8, stride=X)]
    s1x[8:16] = vel1_pad[pl.ds(PAD, 8, stride=X)]
    s1xu[...] = den_pad[pl.ds(PAD + X - 1, 8, stride=X)]
    ends = pack_ends(den)
    lane8 = lanes((8, Y))
    for k in range(K):
        ends = jnp.where(lane8 == 2 * K + k, pltpu.roll(group(vel2, k), 2 * K + k, 1), ends)
    s1y[...] = ends

    pl.semaphore_wait(barrier, 6)

    send(den_pad.at[pl.ds(PAD + R - X, X)], h1.at[pl.ds(0, 16)], 0, zp)
    send(s1z, h1.at[pl.ds(16, 32)], 0, zm)
    send(s1xu, h1.at[pl.ds(48, 8)], 0, xp)
    send(s1x, h1.at[pl.ds(56, 16)], 0, xm)
    send(s1y, h1.at[pl.ds(72, 8)], 0, yp)
    send(s1y, h1.at[pl.ds(80, 8)], 0, ym)
    whole(h1, 0).wait_recv()
    wide = nx == 8 and ny == 8
    if wide:
        for far in ((2, 0), (6, 0), (0, 2), (0, 6)):
            hello(0, *far)
    for step in (2, 6):
        pl.semaphore_signal(
            known.at[2], inc=1, device_id={"gz": lax.rem(iz + step, nz)}, device_id_type=MESH
        )

    def face(first, own, other):
        return jnp.where(first, own, other)

    zb = jnp.concatenate([face(z_first, den[0:X], h1[0:16]), den[: R - X]], axis=0)
    za = jnp.concatenate([den[X:], face(z_last, den[R - X :], h1[16:32])], axis=0)
    bx = spread(h1[48:56], h1[56:64])
    xb = jnp.where(in_x == 0, face(x_first, den, bx), den_pad[PAD - 1 : PAD - 1 + R])
    xa = jnp.where(in_x == X - 1, face(x_last, den, bx), den_pad[PAD + 1 : PAD + 1 + R])
    by = unpack(merge(h1[72:80], h1[80:88]))
    yb = jnp.where(lane == 0, face(y_first, den, by), pltpu.roll(den, 1, 1))
    ya = jnp.where(lane == Y - 1, face(y_last, den, by), pltpu.roll(den, Y - 1, 1))
    low_z, up_z = 2.0 * recip(den + zb), 2.0 * recip(den + za)
    low_x, up_x = 2.0 * recip(den + xb), 2.0 * recip(den + xa)
    low_y, up_y = 2.0 * recip(den + yb), 2.0 * recip(den + ya)
    inverse = recip(low_z + up_z + low_x + up_x + low_y + up_y)

    def keep(flag):
        return jnp.where(flag, 0.0, 1.0)

    zero = jnp.zeros((R, Y), jnp.float32)
    coef[0] = low_z
    coef[1] = low_x
    coef[2] = low_y
    coef[3] = up_z
    coef[4] = jnp.where(in_x == X - 1, 0.0, up_x)
    coef[5] = jnp.where(lane == Y - 1, 0.0, up_y)
    coef[6] = jnp.where(in_x == 0, 0.0, low_x)
    coef[7] = jnp.where(lane == 0, 0.0, low_y)
    coef[8] = jnp.where(
        in_x == 0, low_x * keep(x_first), jnp.where(in_x == X - 1, up_x * keep(x_last), zero)
    )
    coef[9] = jnp.where(
        lane == 0, low_y * keep(y_first), jnp.where(lane == Y - 1, up_y * keep(y_last), zero)
    )
    coef[10] = inverse
    edge_z[0:X] = low_z[0:X] * keep(z_first)
    edge_z[X : 2 * X] = up_z[R - X :] * keep(z_last)

    weights[0] = inverse * coef[8]
    weights[1] = inverse * coef[9]
    weights[2] = zero
    weights[2, 0:X] = inverse[0:X] * edge_z[0:X]
    weights[2, R - X : R] = inverse[R - X :] * edge_z[X : 2 * X]
    for i in range(3):
        stat_z[0, 16 * i : 16 * i + 16] = weights[i, 0:X]
        stat_z[1, 16 * i : 16 * i + 16] = weights[i, R - X : R]
        face_x = weights.at[i]
        stat_x[0, 8 * i : 8 * i + 8] = face_x[pl.ds(0, 8, stride=X)]
        stat_x[1, 8 * i : 8 * i + 8] = face_x[pl.ds(X - 1, 8, stride=X)]
        stat_y[8 * i : 8 * i + 8] = pack_ends(weights[i])
    send(stat_z.at[1], stat.at[pl.ds(0, 48)], 3, zp)
    send(stat_z.at[0], stat.at[pl.ds(48, 48)], 3, zm)
    send(stat_y, stat.at[pl.ds(96, 24)], 3, yp)
    send(stat_y, stat.at[pl.ds(120, 24)], 3, ym)
    send(stat_x.at[1], stat.at[pl.ds(144, 24)], 3, xp)
    send(stat_x.at[0], stat.at[pl.ds(168, 24)], 3, xm)

    above0 = jnp.concatenate([vel0[X:], h1[32:48] * keep(z_last)], axis=0)
    bv = spread(h1[56:64], h1[64:72])
    above1 = jnp.where(in_x == X - 1, bv * keep(x_last), vel1_pad[PAD + 1 : PAD + 1 + R])
    ends_above = h1[80:88]
    bw = jnp.concatenate(
        [pltpu.roll(ends_above, Y - 1 - (2 * K + k), 1) for k in range(K)], axis=0
    )
    above2 = jnp.where(lane == Y - 1, bw * keep(y_last), pltpu.roll(vel2, Y - 1, 1))
    rhs = -(((above0 - vel0) + (above1 - vel1)) + (above2 - vel2))

    def hand_out(buf, recv, group_id, steps):
        rows = buf.shape[1]
        for k in steps:
            to = lax.rem(iz + k, nz)
            send(buf.at[to], recv.at[pl.ds(iz * rows, rows)], group_id, {"gz": to})

    def scatter(fields, buf, recv, group_id, steps):
        for q, ref in enumerate(fields):
            for t in range(TF):
                for r in range(2):
                    at = 16 * q + 8 * r
                    buf[t, at : at + 8] = ref[pl.ds(r * (R // 2) + t, 8, stride=8)]
        rows = 16 * len(fields)
        hand_out(buf, recv, group_id, steps)
        recv[pl.ds(pl.multiple_of(iz * rows, rows), rows)] = buf[iz]

    folded = []

    def fold(value):
        value = jnp.sum(value.reshape(K, 8, Y), axis=0)
        for step in (64, 32, 16):
            value = value + pltpu.roll(value, step, 1)
        m = len(folded)
        before = folded[-1] if folded else jnp.zeros((8, Y), jnp.float32)
        folded.append(jnp.where(lane8 // 16 == m, value, before))

    def gradient(j, v, z_low, x_low, y_low):
        g0, g1, g2 = coef[0] * v - z_low, coef[1] * v - x_low, coef[2] * v - y_low
        grads[j, 0] = g0
        grads[j, 1] = g1
        grads[j, 2] = g2
        grads[j, 3] = g0 + g1 + g2

    def near(axis, here, count, step):
        return {axis: lax.rem(here + count - step, count)}

    edges = (4, 3)
    waits = [pl.ds(0, 128 + 25 * count) for count in edges]

    def exchange(p, own, v, inner):
        nxt = coef[10] * inner
        scaled_v[p] = nxt
        hp = h.at[p]
        for side, at in ((1, R - X), (0, 0)):
            dz[p, side, 0:16] = v[at : at + X]
            dz[p, side, 16:32] = nxt[at : at + X]
        q = pack_ends(v)
        dy[p, 0:8] = q
        dy[p, 8:16] = pack_ends(nxt)
        for side, at in ((1, X - 1), (0, 0)):
            dx[p, side, 0:8] = scaled_v.at[p][pl.ds(at, 8, stride=X)]
            dx[p, side, 8:16] = own[pl.ds(PAD + at, 8, stride=X)]
            dx[p, side, 16:24] = q
        signs = ((-1, -1), (-1, 1), (1, -1), (1, 1))[: edges[p]]
        for i, (a, b) in enumerate(signs):
            row_at = PAD + (R - X if a < 0 else 0) + (X - 1 if b < 0 else 0)
            to = near("gz", iz, nz, a) | near("gx", ix, nx, b)
            send(own.at[pl.ds(row_at, 1)], hp.at[pl.ds(224 + i, 1)], 1 + p, to)
        for i, (a, b) in enumerate(signs):
            to = near("gz", iz, nz, a) | near("gy", iy, ny, b)
            send(dy.at[p, pl.ds(0, 8)], hp.at[pl.ds(128 + 8 * i, 8)], 1 + p, to)
        for i, (a, b) in enumerate(signs):
            to = near("gx", ix, nx, a) | near("gy", iy, ny, b)
            side = 1 if a < 0 else 0
            send(dx.at[p, side, pl.ds(8, 16)], hp.at[pl.ds(160 + 16 * i, 16)], 1 + p, to)
        send(dz.at[p, 1], hp.at[pl.ds(0, 32)], 1 + p, zp)
        send(dz.at[p, 0], hp.at[pl.ds(32, 32)], 1 + p, zm)
        send(dy.at[p], hp.at[pl.ds(96, 16)], 1 + p, yp)
        send(dy.at[p], hp.at[pl.ds(112, 16)], 1 + p, ym)
        send(dx.at[p, 1, pl.ds(0, 16)], hp.at[pl.ds(64, 16)], 1 + p, xp)
        send(dx.at[p, 0, pl.ds(0, 16)], hp.at[pl.ds(80, 16)], 1 + p, xm)

    sub8 = lax.broadcasted_iota(jnp.int32, (8, Y), 0)

    def received(p):
        hp = h.at[p]
        z_faces = (hp[0:16], hp[32:48])
        x_faces = (hp[72:80], hp[88:96])
        return z_faces, x_faces, merge(hp[96:104], hp[112:120])

    def computed(p, v):
        hp = h.at[p]
        low_only = p == 1
        pairs = ((0, 1), (2, 2 if low_only else 3))
        corner = [[hp[224 + i : 225 + i] for i in pair] for pair in pairs]
        zy = [merge(*(hp[128 + 8 * i : 136 + 8 * i] for i in pair)) for pair in pairs]
        xy_rows = [[hp[160 + 16 * i : 168 + 16 * i] for i in pair] for pair in pairs]
        xy = [merge(*(hp[168 + 16 * i : 176 + 16 * i] for i in pair)) for pair in pairs]
        z_faces, x_faces = [], []
        for a, (at, first) in enumerate(((0, 2 * K - 4), (R - X, 0))[: 2 - low_only]):
            from_y = jnp.concatenate(
                [pltpu.roll(zy[a], Y - first - 1, 1), pltpu.roll(zy[a], Y - first - 3, 1)], axis=0
            )
            value = hp[16 + 32 * a : 32 + 32 * a]
            value = value + stat[48 * a + 32 : 48 * a + 48] * v[at : at + X]
            value = value + stat[48 * a : 48 * a + 16] * rows_of(corner[a][0], corner[a][1])
            z_faces.append(value + stat[48 * a + 16 : 48 * a + 32] * from_y)
        for a in range(2 - low_only):
            mine = dx[p, a, 8:16]
            from_z = jnp.where(
                sub8 == 0,
                jnp.broadcast_to(corner[0][a], (8, Y)),
                jnp.broadcast_to(corner[1][a], (8, Y)),
            )
            from_y = jnp.where(
                lane8 == 0, pltpu.roll(xy_rows[a][0], 1, 1), pltpu.roll(xy_rows[a][1], Y - 1, 1)
            )
            at = 144 + 24 * a
            value = hp[64 + 16 * a : 72 + 16 * a] + stat[at : at + 8] * mine
            value = value + stat[at + 8 : at + 16] * from_y
            x_faces.append(value + stat[at + 16 : at + 24] * from_z)
        last_z = 2 * K - 4
        from_z = jnp.where(lane8 < 4, pltpu.roll(zy[0], Y - last_z, 1), pltpu.roll(zy[1], last_z, 1))
        from_x = jnp.where(
            sub8 == 0,
            pltpu.roll(pltpu.roll(xy[0], Y - 2, 1), 1, 0),
            pltpu.roll(pltpu.roll(xy[1], 2, 1), 7, 0),
        )
        both = merge(hp[104:112], hp[120:128])
        both = both + stat_m[8:16] * dy[p, 0:8]
        both = both + stat_m[0:8] * from_x
        return z_faces, x_faces, both + stat_m[16:24] * from_z

    vel_sum[...] = vel0 + vel1 + vel2
    scaled = rhs
    late = None
    for j in range(4):
        p = j // 2
        v = coef[10] * scaled
        own = v_pad.at[j]
        own[PAD : PAD + R] = v
        z_low = coef[0, X:R] * v[: R - X]
        x_low = coef[6] * own[PAD - 1 : PAD - 1 + R]
        y_low = coef[7] * pltpu.roll(v, 1, 1)
        if j < 3:
            z_up = coef[3, 0 : R - X] * v[X:]
            x_up = coef[4] * own[PAD + 1 : PAD + 1 + R]
            y_up = coef[5] * pltpu.roll(v, Y - 1, 1)
            rest = (x_low + x_up) + (y_low + y_up)
        if j % 2 == 0:
            edge = jnp.zeros((X, Y), jnp.float32)
            inner = jnp.concatenate([edge, z_low], axis=0) + jnp.concatenate([z_up, edge], axis=0)
            exchange(p, own, v, inner + rest)
            earlier = late
            if j:
                fold(last[0] * last[4])
                gradient(*earlier)
                gradient(1, *last[:4])
                scatter([vel_sum, grads.at[0, 3], grads.at[1, 3]], send_a, recv_a, 8, FAR_FIRST)
            fold(scaled * v)
            if j == 0:
                if wide:
                    pl.semaphore_wait(known.at[0], 4)
                pl.semaphore_wait(known.at[2], 2)
                whole(stat, 3).wait_recv()
                for i in range(3):
                    stat_m[8 * i : 8 * i + 8] = merge(
                        stat[96 + 8 * i : 104 + 8 * i], stat[120 + 8 * i : 128 + 8 * i]
                    )
            elif wide:
                pl.semaphore_wait(known.at[1], 2)
            whole(h.at[p, waits[p]], 1 + p).wait_recv()
            if wide and j == 0:
                hello(1, 4, 0)
                hello(1, 0, 4)
            z_faces, x_faces, both = received(p)
        else:
            fold(scaled * v)
            z_faces, x_faces, both = following
        z_low = jnp.concatenate([edge_z[0:X] * z_faces[0], z_low], axis=0)
        x_edge = coef[8] * spread(x_faces[0], x_faces[-1])
        y_edge = coef[9] * unpack(both)
        x_low = x_low + jnp.where(in_x == 0, x_edge, 0.0)
        y_low = y_low + jnp.where(lane == 0, y_edge, 0.0)
        if j < 3:
            z_up = jnp.concatenate([z_up, edge_z[X : 2 * X] * z_faces[1]], axis=0)
            scaled = ((z_low + z_up) + rest) + (x_edge + y_edge)
        if j % 2 == 0:
            following = computed(p, v)
            fold(v * scaled)
            late = (j, v, z_low, x_low, y_low)
        elif j == 1:
            last = (v, z_low, x_low, y_low, scaled)
        else:
            fold((2.0 * v) * ((z_low + x_low) + y_low))

    line = jnp.sum(folded[-1], axis=0, keepdims=True)
    row_send[0] = line
    others = [(dx, dy) for dx in range(nx) for dy in range(ny) if dx or dy]

    others.sort(key=lambda apart: ((apart[1] - 1) % ny, -min(apart[0], nx - apart[0])))
    for at, apart in enumerate(others):
        send(row_send.at[0], row_plane.at[pl.ds(at, 1)], 5, in_plane(*apart))
    row_plane[pl.ds(len(others), 1)] = line
    gradient(*late)
    gradient(3, v, z_low, x_low, y_low)
    scatter([grads.at[2, 3], grads.at[3, 3]], send_c, recv_c, 10, FAR_FIRST)
    whole(row_plane.at[pl.ds(0, len(others))], 5).wait_recv()
    line = jnp.sum(row_plane[0 : len(others) + 1], axis=0, keepdims=True)
    row_send[1] = line
    for k in FAR_FIRST:
        send(row_send.at[1], row_line.at[pl.ds(k - 1, 1)], 6, {"gz": lax.rem(iz + k, nz)})
    row_line[nz - 1 : nz] = line
    for ref, group_id in ((recv_a, 8), (recv_c, 10)):
        whole(ref.at[pl.ds(0, ref.shape[0] // nz * (nz - 1))], group_id).wait_recv()
    for copy in params:
        copy.wait()
    whole(row_line.at[pl.ds(0, nz - 1)], 6).wait_recv()
    line = jnp.sum(row_line[...], axis=0, keepdims=True)
    lane1 = lanes((1, Y))
    m = [jnp.sum(jnp.where(lane1 // 16 == i, line, 0.0), axis=1, keepdims=True) for i in range(8)]

    a = [[m[i + j] - m[i + j + 1] for j in range(4)] for i in range(4)]
    b = [m[i] for i in range(4)]
    pivots = []
    for p in range(4):
        ok = a[p][p] > 1e-7 * (m[2 * p] - m[2 * p + 1])
        pivots.append(jnp.where(ok, 1.0 / jnp.where(ok, a[p][p], 1.0), 0.0))
        for i in range(p + 1, 4):
            factor = a[p][i] * pivots[p]
            for j in range(i, 4):
                a[i][j] = a[i][j] - factor * a[p][j]
            b[i] = b[i] - factor * b[p]
    c = [None] * 4
    for p in reversed(range(4)):
        value = b[p]
        for j in range(p + 1, 4):
            value = value - a[p][j] * c[j]
        c[p] = value * pivots[p]

    field = []
    for z in range(Z):
        halves = []
        for r in range(2):
            at = 2 * z + r
            value = recv_a[pl.ds(at, 8, stride=48)]
            value = value - c[0] * recv_a[pl.ds(16 + at, 8, stride=48)]
            value = value - c[1] * recv_a[pl.ds(32 + at, 8, stride=48)]
            value = value - c[2] * recv_c[pl.ds(at, 8, stride=32)]
            value = value - c[3] * recv_c[pl.ds(16 + at, 8, stride=32)]
            halves.append(value)
        field.append(jnp.concatenate(halves, axis=0))
    sub = lax.broadcasted_iota(jnp.int32, (8, Y), 0)
    for k in FAR_FIRST + (0,):
        t = lax.rem(iz + k, nz)
        half = 0.5 / (Z * nz) * gain[t]
        slopes = [0.5 * slope[i, t] for i in range(4)]
        offsets = [0.5 * offset[i, t] for i in range(4)]
        through = jnp.ones((16, Y), jnp.float32)
        colors = [jnp.zeros((16, Y), jnp.float32) for _ in range(3)]
        for z in range(Z):
            weight = through * (half + half * jnp.tanh(slopes[3] * field[z] + offsets[3]))
            through = through - weight
            for i in range(3):
                colors[i] = colors[i] + weight * jnp.tanh(slopes[i] * field[z] + offsets[i])
        lines = [[None, None] for _ in range(4)]
        for r in range(2):
            here = through[8 * r : 8 * r + 8]
            before = jnp.where(sub >= 1, pltpu.roll(here, 1, 0), 1.0)
            for step in (1, 2, 4):
                before = before * jnp.where(sub >= step, pltpu.roll(before, step, 0), 1.0)
            for i in range(3):
                color = 0.5 * (colors[i][8 * r : 8 * r + 8] + (1.0 - here))
                lines[i][r] = jnp.sum(before * color, axis=0, keepdims=True)
            lines[3][r] = (1.0 - before * here)[7:8]
        tile = jnp.concatenate([lines[i][r] for i in range(4) for r in range(2)], axis=0)
        if k:
            img_send[t] = tile
            send(img_send.at[t], img_recv.at[pl.ds(iz * 8, 8)], 11, {"gz": t})
        else:
            img_recv[pl.ds(pl.multiple_of(iz * 8, 8), 8)] = tile
    for d in range(3):
        value = vel_v[d * R : (d + 1) * R]
        for j in range(4):
            value = value - c[j] * grads[j, d]
        corrected[d * R : (d + 1) * R] = value
    whole(img_recv.at[pl.ds(0, 8 * (nz - 1))], 11).wait_recv()
    for i in range(4):
        for r in range(2):
            images[i * X + 8 * r : i * X + 8 * r + 8] = img_recv[pl.ds(2 * i + r, 8, stride=8)]

    whole(h1, 0).wait_send()
    whole(stat, 3).wait_send()
    for p in range(2):
        whole(h.at[p, waits[p]], 1 + p).wait_send()
    whole(row_plane.at[pl.ds(0, len(others))], 5).wait_send()
    whole(row_line.at[pl.ds(0, nz - 1)], 6).wait_send()
    for ref, group_id in ((recv_a, 8), (recv_c, 10), (img_recv, 11)):
        whole(ref.at[pl.ds(0, ref.shape[0] // nz * (nz - 1))], group_id).wait_send()


def write_out(corrected, images, corrected_out, images_out, sem):
    copies = [
        pltpu.make_async_copy(corrected, corrected_out, sem.at[0]),
        pltpu.make_async_copy(images, images_out, sem.at[1]),
    ]
    for copy in copies:
        copy.start()
    for copy in copies:
        copy.wait()


def local(sizes, phase_field, thermal, velocity, transfer_slope, transfer_offset, transfer_gain):
    f32 = jnp.float32
    hbm = pl.BlockSpec(memory_space=pltpu.HBM)
    vmem = pl.BlockSpec(memory_space=pltpu.VMEM)
    corrected, images = pl.pallas_call(
        functools.partial(kernel, sizes),
        out_shape=(
            jax.ShapeDtypeStruct((3 * R, Y), f32),
            jax.ShapeDtypeStruct((4 * X, Y), f32),
        ),
        in_specs=[hbm] * 6,
        out_specs=(vmem, vmem),
        scratch_shapes=[
            pltpu.SMEM((4, TF), f32),
            pltpu.SMEM((4, TF), f32),
            pltpu.SMEM((TF,), f32),
            pltpu.VMEM((R, Y), jnp.int32),
            pltpu.VMEM((R, Y), f32),
            pltpu.VMEM((3 * R, Y), f32),
            pltpu.VMEM((R + 2 * PAD, Y), f32),
            pltpu.VMEM((R + 2 * PAD, Y), f32),
            pltpu.VMEM((2 * X, Y), f32),
            pltpu.VMEM((16, Y), f32),
            pltpu.VMEM((8, Y), f32),
            pltpu.VMEM((8, Y), f32),
            pltpu.VMEM((88, Y), f32),
            pltpu.VMEM((4, R + 2 * PAD, Y), f32),
            pltpu.VMEM((11, R, Y), f32),
            pltpu.VMEM((2 * X, Y), f32),
            pltpu.VMEM((3, R, Y), f32),
            pltpu.VMEM((2, 48, Y), f32),
            pltpu.VMEM((2, 24, Y), f32),
            pltpu.VMEM((24, Y), f32),
            pltpu.VMEM((192, Y), f32),
            pltpu.VMEM((24, Y), f32),
            pltpu.VMEM((2, R, Y), f32),
            pltpu.VMEM((2, 2, 32, Y), f32),
            pltpu.VMEM((2, 2, 24, Y), f32),
            pltpu.VMEM((2, 16, Y), f32),
            pltpu.VMEM((2, 232, Y), f32),
            pltpu.VMEM((4, 4, R, Y), f32),
            pltpu.VMEM((2, 1, Y), f32),
            pltpu.VMEM((sizes[0] * sizes[1], Y), f32),
            pltpu.VMEM((sizes[2], Y), f32),
            pltpu.VMEM((TF, 48, Y), f32),
            pltpu.VMEM((TF, 32, Y), f32),
            pltpu.VMEM((TF * 48, Y), f32),
            pltpu.VMEM((TF * 32, Y), f32),
            pltpu.VMEM((R, Y), f32),
            pltpu.VMEM((TF, 8, Y), f32),
            pltpu.VMEM((TF * 8, Y), f32),
            pltpu.SemaphoreType.DMA((6,)),
            pltpu.SemaphoreType.DMA((12,)),
            pltpu.SemaphoreType.DMA((12,)),
            pltpu.SemaphoreType.REGULAR((3,)),
        ],
        compiler_params=pltpu.CompilerParams(
            collective_id=0, has_side_effects=True, vmem_limit_bytes=16 * 2**20
        ),
    )(
        *(
            pltpu.with_memory_space_constraint(value, pltpu.HBM)
            for value in (
                phase_field.reshape(R, Y),
                thermal.reshape(R, Y),
                velocity.reshape(3 * R, Y),
                transfer_slope.T,
                transfer_offset.T,
                transfer_gain,
            )
        )
    )
    corrected, images = pl.pallas_call(
        write_out,
        out_shape=(
            jax.ShapeDtypeStruct((3 * R, Y), f32),
            jax.ShapeDtypeStruct((4 * X, Y), f32),
        ),
        in_specs=[vmem, vmem],
        out_specs=(hbm, hbm),
        scratch_shapes=[pltpu.SemaphoreType.DMA((2,))],
        compiler_params=pltpu.CompilerParams(vmem_limit_bytes=2 * 2**20),
    )(corrected, images)
    return corrected.reshape(3, Z, X, Y), images.reshape(1, 4, X, Y)


def solution(mesh):
    sizes = (mesh.shape["gx"], mesh.shape["gy"], mesh.shape["gz"])
    return jax.shard_map(
        functools.partial(local, sizes),
        mesh=mesh,
        in_specs=(
            P("gz", "gx", "gy"),
            P("gz", "gx", "gy"),
            P(None, "gz", "gx", "gy"),
            P(),
            P(),
            P(),
        ),
        out_specs=(P(None, "gz", "gx", "gy"), P("gz", None, "gx", "gy")),
        check_vma=False,
    )
```

```python
import functools

import jax
import jax.numpy as jnp
from jax import lax
from jax.experimental import pallas as pl
from jax.experimental.pallas import tpu as pltpu
from jax.sharding import PartitionSpec as P

MESH = pl.DeviceIdType.MESH
Z, X, Y = 8, 16, 128
R = Z * X
K = R // 8
TF = 8
PAD = 8
FAR_FIRST = (4, 3, 5, 2, 6, 1, 7)


def lanes(shape):
    return lax.broadcasted_iota(jnp.int32, shape, 1)


def group(v, k):
    return v[8 * k : 8 * k + 8]


def recip(v):
    r = pl.reciprocal(v, approx=True)
    r = r * (2.0 - v * r)
    return r * (2.0 - v * r)


def pack_ends(v):
    lane = lanes((8, Y))
    out = jnp.zeros((8, Y), jnp.float32)
    for k in range(K):
        out = jnp.where(lane // 2 == k, pltpu.roll(group(v, k), 2 * k + 1, 1), out)
    return out


def merge(below, above):
    even = lanes((8, Y)) % 2 == 0
    return jnp.where(even, pltpu.roll(above, Y - 1, 1), pltpu.roll(below, 1, 1))


def unpack(both):
    return jnp.concatenate([pltpu.roll(both, Y - (2 * k + 1), 1) for k in range(K)], axis=0)


def rows_of(first, second):
    return jnp.concatenate(
        [jnp.broadcast_to(first, (8, Y)), jnp.broadcast_to(second, (8, Y))], axis=0
    )


def spread(below, above):
    pieces = []
    for z in range(Z):
        pieces.append(jnp.broadcast_to(below[z : z + 1], (8, Y)))
        pieces.append(jnp.broadcast_to(above[z : z + 1], (8, Y)))
    return jnp.concatenate(pieces, axis=0)


def kernel(
    sizes,
    phase_in,
    thermal_in,
    vel_in,
    slope_in,
    offset_in,
    gain_in,
    corrected,
    images,
    slope,
    offset,
    gain,
    phase_v,
    thermal_v,
    vel_v,
    vel1_pad,
    den_pad,
    s1z,
    s1x,
    s1xu,
    s1y,
    h1,
    v_pad,
    coef,
    edge_z,
    weights,
    stat_z,
    stat_x,
    stat_y,
    stat,
    stat_m,
    scaled_v,
    dz,
    dx,
    dy,
    h,
    grads,
    row_send,
    row_plane,
    row_line,
    send_a,
    send_c,
    recv_a,
    recv_c,
    vel_sum,
    img_send,
    img_recv,
    in_sem,
    send_sem,
    recv_sem,
    known,
):
    nx, ny, nz = sizes
    ix, iy, iz = lax.axis_index("gx"), lax.axis_index("gy"), lax.axis_index("gz")
    xm, xp = {"gx": lax.rem(ix + nx - 1, nx)}, {"gx": lax.rem(ix + 1, nx)}
    ym, yp = {"gy": lax.rem(iy + ny - 1, ny)}, {"gy": lax.rem(iy + 1, ny)}
    zm, zp = {"gz": lax.rem(iz + nz - 1, nz)}, {"gz": lax.rem(iz + 1, nz)}
    x_first, x_last = ix == 0, ix == nx - 1
    y_first, y_last = iy == 0, iy == ny - 1
    z_first, z_last = iz == 0, iz == nz - 1

    loads = [
        pltpu.make_async_copy(phase_in, phase_v, in_sem.at[0]),
        pltpu.make_async_copy(thermal_in, thermal_v, in_sem.at[1]),
        pltpu.make_async_copy(vel_in, vel_v, in_sem.at[2]),
    ]
    params = [
        pltpu.make_async_copy(slope_in, slope, in_sem.at[3]),
        pltpu.make_async_copy(offset_in, offset, in_sem.at[4]),
        pltpu.make_async_copy(gain_in, gain, in_sem.at[5]),
    ]
    for copy in loads:
        copy.start()
    barrier = pltpu.get_barrier_semaphore()
    for device in (zm, zp, ym, yp, xm, xp):
        pl.semaphore_signal(barrier, inc=1, device_id=device, device_id_type=MESH)
    for copy in params:
        copy.start()

    pad = jnp.zeros((PAD, Y), jnp.float32)
    for ref in [den_pad, vel1_pad] + [v_pad.at[j] for j in range(4)]:
        ref[0:PAD] = pad
        ref[PAD + R : PAD + R + PAD] = pad

    def send(src, dst, group_id, device):
        pltpu.make_async_remote_copy(
            src, dst, send_sem.at[group_id], recv_sem.at[group_id], device_id=device, device_id_type=MESH
        ).start()

    def whole(ref, group_id):
        return pltpu.make_async_remote_copy(
            ref, ref, send_sem.at[group_id], recv_sem.at[group_id], device_id=xp, device_id_type=MESH
        )

    def in_plane(dx, dy):
        return {"gx": lax.rem(ix + dx, nx), "gy": lax.rem(iy + dy, ny)}

    def hello(which, dx, dy):
        pl.semaphore_signal(
            known.at[which], inc=1, device_id=in_plane(dx, dy), device_id_type=MESH
        )

    lane = lanes((R, Y))
    row = lax.broadcasted_iota(jnp.int32, (R, Y), 0)
    in_x = row % X

    for copy in loads:
        copy.wait()
    den = (1.0 + 9.0 * phase_v[...].astype(jnp.float32)) * thermal_v[...]
    den_pad[PAD : PAD + R] = den
    vel0, vel1, vel2 = vel_v[0:R], vel_v[R : 2 * R], vel_v[2 * R : 3 * R]
    vel1_pad[PAD : PAD + R] = vel1
    s1z[0:X] = den[0:X]
    s1z[X : 2 * X] = vel0[0:X]
    s1x[0:8] = den_pad[pl.ds(PAD, 8, stride=X)]
    s1x[8:16] = vel1_pad[pl.ds(PAD, 8, stride=X)]
    s1xu[...] = den_pad[pl.ds(PAD + X - 1, 8, stride=X)]
    ends = pack_ends(den)
    lane8 = lanes((8, Y))
    for k in range(K):
        ends = jnp.where(lane8 == 2 * K + k, pltpu.roll(group(vel2, k), 2 * K + k, 1), ends)
    s1y[...] = ends

    pl.semaphore_wait(barrier, 6)

    send(den_pad.at[pl.ds(PAD + R - X, X)], h1.at[pl.ds(0, 16)], 0, zp)
    send(s1z, h1.at[pl.ds(16, 32)], 0, zm)
    send(s1xu, h1.at[pl.ds(48, 8)], 0, xp)
    send(s1x, h1.at[pl.ds(56, 16)], 0, xm)
    send(s1y, h1.at[pl.ds(72, 8)], 0, yp)
    send(s1y, h1.at[pl.ds(80, 8)], 0, ym)
    whole(h1, 0).wait_recv()
    wide = nx == 8 and ny == 8
    if wide:
        for far in ((2, 0), (6, 0), (0, 2), (0, 6)):
            hello(0, *far)
    for step in (2, 6):
        pl.semaphore_signal(
            known.at[2], inc=1, device_id={"gz": lax.rem(iz + step, nz)}, device_id_type=MESH
        )

    def face(first, own, other):
        return jnp.where(first, own, other)

    zb = jnp.concatenate([face(z_first, den[0:X], h1[0:16]), den[: R - X]], axis=0)
    za = jnp.concatenate([den[X:], face(z_last, den[R - X :], h1[16:32])], axis=0)
    bx = spread(h1[48:56], h1[56:64])
    xb = jnp.where(in_x == 0, face(x_first, den, bx), den_pad[PAD - 1 : PAD - 1 + R])
    xa = jnp.where(in_x == X - 1, face(x_last, den, bx), den_pad[PAD + 1 : PAD + 1 + R])
    by = unpack(merge(h1[72:80], h1[80:88]))
    yb = jnp.where(lane == 0, face(y_first, den, by), pltpu.roll(den, 1, 1))
    ya = jnp.where(lane == Y - 1, face(y_last, den, by), pltpu.roll(den, Y - 1, 1))
    low_z, up_z = 2.0 * recip(den + zb), 2.0 * recip(den + za)
    low_x, up_x = 2.0 * recip(den + xb), 2.0 * recip(den + xa)
    low_y, up_y = 2.0 * recip(den + yb), 2.0 * recip(den + ya)
    inverse = recip(low_z + up_z + low_x + up_x + low_y + up_y)

    def keep(flag):
        return jnp.where(flag, 0.0, 1.0)

    zero = jnp.zeros((R, Y), jnp.float32)
    coef[0] = low_z
    coef[1] = low_x
    coef[2] = low_y
    coef[3] = up_z
    coef[4] = jnp.where(in_x == X - 1, 0.0, up_x)
    coef[5] = jnp.where(lane == Y - 1, 0.0, up_y)
    coef[6] = jnp.where(in_x == 0, 0.0, low_x)
    coef[7] = jnp.where(lane == 0, 0.0, low_y)
    coef[8] = jnp.where(
        in_x == 0, low_x * keep(x_first), jnp.where(in_x == X - 1, up_x * keep(x_last), zero)
    )
    coef[9] = jnp.where(
        lane == 0, low_y * keep(y_first), jnp.where(lane == Y - 1, up_y * keep(y_last), zero)
    )
    coef[10] = inverse
    edge_z[0:X] = low_z[0:X] * keep(z_first)
    edge_z[X : 2 * X] = up_z[R - X :] * keep(z_last)

    weights[0] = inverse * coef[8]
    weights[1] = inverse * coef[9]
    weights[2] = zero
    weights[2, 0:X] = inverse[0:X] * edge_z[0:X]
    weights[2, R - X : R] = inverse[R - X :] * edge_z[X : 2 * X]
    for i in range(3):
        stat_z[0, 16 * i : 16 * i + 16] = weights[i, 0:X]
        stat_z[1, 16 * i : 16 * i + 16] = weights[i, R - X : R]
        face_x = weights.at[i]
        stat_x[0, 8 * i : 8 * i + 8] = face_x[pl.ds(0, 8, stride=X)]
        stat_x[1, 8 * i : 8 * i + 8] = face_x[pl.ds(X - 1, 8, stride=X)]
        stat_y[8 * i : 8 * i + 8] = pack_ends(weights[i])
    send(stat_z.at[1], stat.at[pl.ds(0, 48)], 3, zp)
    send(stat_z.at[0], stat.at[pl.ds(48, 48)], 3, zm)
    send(stat_y, stat.at[pl.ds(96, 24)], 3, yp)
    send(stat_y, stat.at[pl.ds(120, 24)], 3, ym)
    send(stat_x.at[1], stat.at[pl.ds(144, 24)], 3, xp)
    send(stat_x.at[0], stat.at[pl.ds(168, 24)], 3, xm)

    above0 = jnp.concatenate([vel0[X:], h1[32:48] * keep(z_last)], axis=0)
    bv = spread(h1[56:64], h1[64:72])
    above1 = jnp.where(in_x == X - 1, bv * keep(x_last), vel1_pad[PAD + 1 : PAD + 1 + R])
    ends_above = h1[80:88]
    bw = jnp.concatenate(
        [pltpu.roll(ends_above, Y - 1 - (2 * K + k), 1) for k in range(K)], axis=0
    )
    above2 = jnp.where(lane == Y - 1, bw * keep(y_last), pltpu.roll(vel2, Y - 1, 1))
    rhs = -(((above0 - vel0) + (above1 - vel1)) + (above2 - vel2))

    def hand_out(buf, recv, group_id, steps):
        rows = buf.shape[1]
        for k in steps:
            to = lax.rem(iz + k, nz)
            send(buf.at[to], recv.at[pl.ds(iz * rows, rows)], group_id, {"gz": to})

    def scatter(fields, buf, recv, group_id, steps):
        for q, ref in enumerate(fields):
            for t in range(TF):
                for r in range(2):
                    at = 16 * q + 8 * r
                    buf[t, at : at + 8] = ref[pl.ds(r * (R // 2) + t, 8, stride=8)]
        rows = 16 * len(fields)
        hand_out(buf, recv, group_id, steps)
        recv[pl.ds(pl.multiple_of(iz * rows, rows), rows)] = buf[iz]

    folded = []

    def fold(value):
        value = jnp.sum(value.reshape(K, 8, Y), axis=0)
        for step in (64, 32, 16):
            value = value + pltpu.roll(value, step, 1)
        m = len(folded)
        before = folded[-1] if folded else jnp.zeros((8, Y), jnp.float32)
        folded.append(jnp.where(lane8 // 16 == m, value, before))

    def gradient(j, v, z_low, x_low, y_low):
        g0, g1, g2 = coef[0] * v - z_low, coef[1] * v - x_low, coef[2] * v - y_low
        grads[j, 0] = g0
        grads[j, 1] = g1
        grads[j, 2] = g2
        grads[j, 3] = g0 + g1 + g2

    def near(axis, here, count, step):
        return {axis: lax.rem(here + count - step, count)}

    edges = (4, 3)
    waits = [pl.ds(0, 128 + 25 * count) for count in edges]

    def exchange(p, own, v, inner):
        nxt = coef[10] * inner
        scaled_v[p] = nxt
        hp = h.at[p]
        for side, at in ((1, R - X), (0, 0)):
            dz[p, side, 0:16] = v[at : at + X]
            dz[p, side, 16:32] = nxt[at : at + X]
        q = pack_ends(v)
        dy[p, 0:8] = q
        dy[p, 8:16] = pack_ends(nxt)
        for side, at in ((1, X - 1), (0, 0)):
            dx[p, side, 0:8] = scaled_v.at[p][pl.ds(at, 8, stride=X)]
            dx[p, side, 8:16] = own[pl.ds(PAD + at, 8, stride=X)]
            dx[p, side, 16:24] = q
        signs = ((-1, -1), (-1, 1), (1, -1), (1, 1))[: edges[p]]
        for i, (a, b) in enumerate(signs):
            row_at = PAD + (R - X if a < 0 else 0) + (X - 1 if b < 0 else 0)
            to = near("gz", iz, nz, a) | near("gx", ix, nx, b)
            send(own.at[pl.ds(row_at, 1)], hp.at[pl.ds(224 + i, 1)], 1 + p, to)
        for i, (a, b) in enumerate(signs):
            to = near("gz", iz, nz, a) | near("gy", iy, ny, b)
            send(dy.at[p, pl.ds(0, 8)], hp.at[pl.ds(128 + 8 * i, 8)], 1 + p, to)
        for i, (a, b) in enumerate(signs):
            to = near("gx", ix, nx, a) | near("gy", iy, ny, b)
            side = 1 if a < 0 else 0
            send(dx.at[p, side, pl.ds(8, 16)], hp.at[pl.ds(160 + 16 * i, 16)], 1 + p, to)
        send(dz.at[p, 1], hp.at[pl.ds(0, 32)], 1 + p, zp)
        send(dz.at[p, 0], hp.at[pl.ds(32, 32)], 1 + p, zm)
        send(dy.at[p], hp.at[pl.ds(96, 16)], 1 + p, yp)
        send(dy.at[p], hp.at[pl.ds(112, 16)], 1 + p, ym)
        send(dx.at[p, 1, pl.ds(0, 16)], hp.at[pl.ds(64, 16)], 1 + p, xp)
        send(dx.at[p, 0, pl.ds(0, 16)], hp.at[pl.ds(80, 16)], 1 + p, xm)

    sub8 = lax.broadcasted_iota(jnp.int32, (8, Y), 0)

    def received(p):
        hp = h.at[p]
        z_faces = (hp[0:16], hp[32:48])
        x_faces = (hp[72:80], hp[88:96])
        return z_faces, x_faces, merge(hp[96:104], hp[112:120])

    def computed(p, v):
        hp = h.at[p]
        low_only = p == 1
        pairs = ((0, 1), (2, 2 if low_only else 3))
        corner = [[hp[224 + i : 225 + i] for i in pair] for pair in pairs]
        zy = [merge(*(hp[128 + 8 * i : 136 + 8 * i] for i in pair)) for pair in pairs]
        xy_rows = [[hp[160 + 16 * i : 168 + 16 * i] for i in pair] for pair in pairs]
        xy = [merge(*(hp[168 + 16 * i : 176 + 16 * i] for i in pair)) for pair in pairs]
        z_faces, x_faces = [], []
        for a, (at, first) in enumerate(((0, 2 * K - 4), (R - X, 0))[: 2 - low_only]):
            from_y = jnp.concatenate(
                [pltpu.roll(zy[a], Y - first - 1, 1), pltpu.roll(zy[a], Y - first - 3, 1)], axis=0
            )
            value = hp[16 + 32 * a : 32 + 32 * a]
            value = value + stat[48 * a + 32 : 48 * a + 48] * v[at : at + X]
            value = value + stat[48 * a : 48 * a + 16] * rows_of(corner[a][0], corner[a][1])
            z_faces.append(value + stat[48 * a + 16 : 48 * a + 32] * from_y)
        for a in range(2 - low_only):
            mine = dx[p, a, 8:16]
            from_z = jnp.where(
                sub8 == 0,
                jnp.broadcast_to(corner[0][a], (8, Y)),
                jnp.broadcast_to(corner[1][a], (8, Y)),
            )
            from_y = jnp.where(
                lane8 == 0, pltpu.roll(xy_rows[a][0], 1, 1), pltpu.roll(xy_rows[a][1], Y - 1, 1)
            )
            at = 144 + 24 * a
            value = hp[64 + 16 * a : 72 + 16 * a] + stat[at : at + 8] * mine
            value = value + stat[at + 8 : at + 16] * from_y
            x_faces.append(value + stat[at + 16 : at + 24] * from_z)
        last_z = 2 * K - 4
        from_z = jnp.where(lane8 < 4, pltpu.roll(zy[0], Y - last_z, 1), pltpu.roll(zy[1], last_z, 1))
        from_x = jnp.where(
            sub8 == 0,
            pltpu.roll(pltpu.roll(xy[0], Y - 2, 1), 1, 0),
            pltpu.roll(pltpu.roll(xy[1], 2, 1), 7, 0),
        )
        both = merge(hp[104:112], hp[120:128])
        both = both + stat_m[8:16] * dy[p, 0:8]
        both = both + stat_m[0:8] * from_x
        return z_faces, x_faces, both + stat_m[16:24] * from_z

    vel_sum[...] = vel0 + vel1 + vel2
    scaled = rhs
    late = None
    for j in range(4):
        p = j // 2
        v = coef[10] * scaled
        own = v_pad.at[j]
        own[PAD : PAD + R] = v
        z_low = coef[0, X:R] * v[: R - X]
        x_low = coef[6] * own[PAD - 1 : PAD - 1 + R]
        y_low = coef[7] * pltpu.roll(v, 1, 1)
        if j < 3:
            z_up = coef[3, 0 : R - X] * v[X:]
            x_up = coef[4] * own[PAD + 1 : PAD + 1 + R]
            y_up = coef[5] * pltpu.roll(v, Y - 1, 1)
            rest = (x_low + x_up) + (y_low + y_up)
        if j % 2 == 0:
            edge = jnp.zeros((X, Y), jnp.float32)
            inner = jnp.concatenate([edge, z_low], axis=0) + jnp.concatenate([z_up, edge], axis=0)
            exchange(p, own, v, inner + rest)
            earlier = late
            if j:
                step_v = last[0] - v
                fold(last[5] * step_v)
                fold(last[4] * step_v)
                gradient(*earlier)
                gradient(1, *last[:4])
                scatter([vel_sum, grads.at[0, 3], grads.at[1, 3]], send_a, recv_a, 8, FAR_FIRST)
            if j == 0:
                fold(scaled * v)
                if wide:
                    pl.semaphore_wait(known.at[0], 4)
                pl.semaphore_wait(known.at[2], 2)
                whole(stat, 3).wait_recv()
                for i in range(3):
                    stat_m[8 * i : 8 * i + 8] = merge(
                        stat[96 + 8 * i : 104 + 8 * i], stat[120 + 8 * i : 128 + 8 * i]
                    )
            elif wide:
                pl.semaphore_wait(known.at[1], 2)
            whole(h.at[p, waits[p]], 1 + p).wait_recv()
            if wide and j == 0:
                hello(1, 4, 0)
                hello(1, 0, 4)
            z_faces, x_faces, both = received(p)
        else:
            step_v = prior[0] - v
            fold(prior[1] * step_v)
            fold(scaled * step_v)
            z_faces, x_faces, both = following
        z_low = jnp.concatenate([edge_z[0:X] * z_faces[0], z_low], axis=0)
        x_edge = coef[8] * spread(x_faces[0], x_faces[-1])
        y_edge = coef[9] * unpack(both)
        x_low = x_low + jnp.where(in_x == 0, x_edge, 0.0)
        y_low = y_low + jnp.where(lane == 0, y_edge, 0.0)
        prior = (v, scaled)
        if j < 3:
            z_up = jnp.concatenate([z_up, edge_z[X : 2 * X] * z_faces[1]], axis=0)
            scaled = ((z_low + z_up) + rest) + (x_edge + y_edge)
        if j % 2 == 0:
            following = computed(p, v)
            late = (j, v, z_low, x_low, y_low)
        elif j == 1:
            last = (v, z_low, x_low, y_low, scaled, prior[1])
        else:
            fold(v * (scaled - 2.0 * ((z_low + x_low) + y_low)))

    line = jnp.sum(folded[-1], axis=0, keepdims=True)
    row_send[0] = line
    others = [(dx, dy) for dx in range(nx) for dy in range(ny) if dx or dy]

    others.sort(key=lambda apart: ((apart[1] - 1) % ny, -min(apart[0], nx - apart[0])))
    for at, apart in enumerate(others):
        send(row_send.at[0], row_plane.at[pl.ds(at, 1)], 5, in_plane(*apart))
    row_plane[pl.ds(len(others), 1)] = line
    gradient(*late)
    gradient(3, v, z_low, x_low, y_low)
    scatter([grads.at[2, 3], grads.at[3, 3]], send_c, recv_c, 10, FAR_FIRST)
    whole(row_plane.at[pl.ds(0, len(others))], 5).wait_recv()
    line = jnp.sum(row_plane[0 : len(others) + 1], axis=0, keepdims=True)
    row_send[1] = line
    for k in FAR_FIRST:
        send(row_send.at[1], row_line.at[pl.ds(k - 1, 1)], 6, {"gz": lax.rem(iz + k, nz)})
    row_line[nz - 1 : nz] = line
    for ref, group_id in ((recv_a, 8), (recv_c, 10)):
        whole(ref.at[pl.ds(0, ref.shape[0] // nz * (nz - 1))], group_id).wait_recv()
    for copy in params:
        copy.wait()
    whole(row_line.at[pl.ds(0, nz - 1)], 6).wait_recv()
    line = jnp.sum(row_line[...], axis=0, keepdims=True)
    lane1 = lanes((1, Y))
    m = [jnp.sum(jnp.where(lane1 // 16 == i, line, 0.0), axis=1, keepdims=True) for i in range(8)]

    drop = m[1:]
    a = [[drop[i + j] for j in range(4)] for i in range(4)]
    b = [m[0]]
    for i in range(3):
        b.append(b[i] - drop[i])
    pivots = []
    for p in range(4):
        ok = a[p][p] > 1e-7 * drop[2 * p]
        pivots.append(jnp.where(ok, 1.0 / jnp.where(ok, a[p][p], 1.0), 0.0))
        for i in range(p + 1, 4):
            factor = a[p][i] * pivots[p]
            for j in range(i, 4):
                a[i][j] = a[i][j] - factor * a[p][j]
            b[i] = b[i] - factor * b[p]
    c = [None] * 4
    for p in reversed(range(4)):
        value = b[p]
        for j in range(p + 1, 4):
            value = value - a[p][j] * c[j]
        c[p] = value * pivots[p]

    field = []
    for z in range(Z):
        halves = []
        for r in range(2):
            at = 2 * z + r
            value = recv_a[pl.ds(at, 8, stride=48)]
            value = value - c[0] * recv_a[pl.ds(16 + at, 8, stride=48)]
            value = value - c[1] * recv_a[pl.ds(32 + at, 8, stride=48)]
            value = value - c[2] * recv_c[pl.ds(at, 8, stride=32)]
            value = value - c[3] * recv_c[pl.ds(16 + at, 8, stride=32)]
            halves.append(value)
        field.append(jnp.concatenate(halves, axis=0))
    sub = lax.broadcasted_iota(jnp.int32, (8, Y), 0)
    for k in FAR_FIRST + (0,):
        t = lax.rem(iz + k, nz)
        half = 0.5 / (Z * nz) * gain[t]
        slopes = [0.5 * slope[i, t] for i in range(4)]
        offsets = [0.5 * offset[i, t] for i in range(4)]
        through = jnp.ones((16, Y), jnp.float32)
        colors = [jnp.zeros((16, Y), jnp.float32) for _ in range(3)]
        for z in range(Z):
            weight = through * (half + half * jnp.tanh(slopes[3] * field[z] + offsets[3]))
            through = through - weight
            for i in range(3):
                colors[i] = colors[i] + weight * jnp.tanh(slopes[i] * field[z] + offsets[i])
        lines = [[None, None] for _ in range(4)]
        for r in range(2):
            here = through[8 * r : 8 * r + 8]
            before = jnp.where(sub >= 1, pltpu.roll(here, 1, 0), 1.0)
            for step in (1, 2, 4):
                before = before * jnp.where(sub >= step, pltpu.roll(before, step, 0), 1.0)
            for i in range(3):
                color = 0.5 * (colors[i][8 * r : 8 * r + 8] + (1.0 - here))
                lines[i][r] = jnp.sum(before * color, axis=0, keepdims=True)
            lines[3][r] = (1.0 - before * here)[7:8]
        tile = jnp.concatenate([lines[i][r] for i in range(4) for r in range(2)], axis=0)
        if k:
            img_send[t] = tile
            send(img_send.at[t], img_recv.at[pl.ds(iz * 8, 8)], 11, {"gz": t})
        else:
            img_recv[pl.ds(pl.multiple_of(iz * 8, 8), 8)] = tile
    for d in range(3):
        value = vel_v[d * R : (d + 1) * R]
        for j in range(4):
            value = value - c[j] * grads[j, d]
        corrected[d * R : (d + 1) * R] = value
    whole(h1, 0).wait_send()
    whole(stat, 3).wait_send()
    for p in range(2):
        whole(h.at[p, waits[p]], 1 + p).wait_send()
    whole(row_plane.at[pl.ds(0, len(others))], 5).wait_send()
    whole(row_line.at[pl.ds(0, nz - 1)], 6).wait_send()
    for ref, group_id in ((recv_a, 8), (recv_c, 10)):
        whole(ref.at[pl.ds(0, ref.shape[0] // nz * (nz - 1))], group_id).wait_send()
    whole(img_recv.at[pl.ds(0, 8 * (nz - 1))], 11).wait_recv()
    whole(img_recv.at[pl.ds(0, 8 * (nz - 1))], 11).wait_send()
    for i in range(4):
        for r in range(2):
            images[i * X + 8 * r : i * X + 8 * r + 8] = img_recv[pl.ds(2 * i + r, 8, stride=8)]


def write_out(corrected, images, corrected_out, images_out, sem):
    copies = [
        pltpu.make_async_copy(corrected, corrected_out, sem.at[0]),
        pltpu.make_async_copy(images, images_out, sem.at[1]),
    ]
    for copy in copies:
        copy.start()
    for copy in copies:
        copy.wait()


def local(sizes, phase_field, thermal, velocity, transfer_slope, transfer_offset, transfer_gain):
    f32 = jnp.float32
    hbm = pl.BlockSpec(memory_space=pltpu.HBM)
    vmem = pl.BlockSpec(memory_space=pltpu.VMEM)
    corrected, images = pl.pallas_call(
        functools.partial(kernel, sizes),
        out_shape=(
            jax.ShapeDtypeStruct((3 * R, Y), f32),
            jax.ShapeDtypeStruct((4 * X, Y), f32),
        ),
        in_specs=[hbm] * 6,
        out_specs=(vmem, vmem),
        scratch_shapes=[
            pltpu.SMEM((4, TF), f32),
            pltpu.SMEM((4, TF), f32),
            pltpu.SMEM((TF,), f32),
            pltpu.VMEM((R, Y), jnp.int32),
            pltpu.VMEM((R, Y), f32),
            pltpu.VMEM((3 * R, Y), f32),
            pltpu.VMEM((R + 2 * PAD, Y), f32),
            pltpu.VMEM((R + 2 * PAD, Y), f32),
            pltpu.VMEM((2 * X, Y), f32),
            pltpu.VMEM((16, Y), f32),
            pltpu.VMEM((8, Y), f32),
            pltpu.VMEM((8, Y), f32),
            pltpu.VMEM((88, Y), f32),
            pltpu.VMEM((4, R + 2 * PAD, Y), f32),
            pltpu.VMEM((11, R, Y), f32),
            pltpu.VMEM((2 * X, Y), f32),
            pltpu.VMEM((3, R, Y), f32),
            pltpu.VMEM((2, 48, Y), f32),
            pltpu.VMEM((2, 24, Y), f32),
            pltpu.VMEM((24, Y), f32),
            pltpu.VMEM((192, Y), f32),
            pltpu.VMEM((24, Y), f32),
            pltpu.VMEM((2, R, Y), f32),
            pltpu.VMEM((2, 2, 32, Y), f32),
            pltpu.VMEM((2, 2, 24, Y), f32),
            pltpu.VMEM((2, 16, Y), f32),
            pltpu.VMEM((2, 232, Y), f32),
            pltpu.VMEM((4, 4, R, Y), f32),
            pltpu.VMEM((2, 1, Y), f32),
            pltpu.VMEM((sizes[0] * sizes[1], Y), f32),
            pltpu.VMEM((sizes[2], Y), f32),
            pltpu.VMEM((TF, 48, Y), f32),
            pltpu.VMEM((TF, 32, Y), f32),
            pltpu.VMEM((TF * 48, Y), f32),
            pltpu.VMEM((TF * 32, Y), f32),
            pltpu.VMEM((R, Y), f32),
            pltpu.VMEM((TF, 8, Y), f32),
            pltpu.VMEM((TF * 8, Y), f32),
            pltpu.SemaphoreType.DMA((6,)),
            pltpu.SemaphoreType.DMA((12,)),
            pltpu.SemaphoreType.DMA((12,)),
            pltpu.SemaphoreType.REGULAR((3,)),
        ],
        compiler_params=pltpu.CompilerParams(
            collective_id=0, has_side_effects=True, vmem_limit_bytes=16 * 2**20
        ),
    )(
        *(
            pltpu.with_memory_space_constraint(value, pltpu.HBM)
            for value in (
                phase_field.reshape(R, Y),
                thermal.reshape(R, Y),
                velocity.reshape(3 * R, Y),
                transfer_slope.T,
                transfer_offset.T,
                transfer_gain,
            )
        )
    )
    corrected, images = pl.pallas_call(
        write_out,
        out_shape=(
            jax.ShapeDtypeStruct((3 * R, Y), f32),
            jax.ShapeDtypeStruct((4 * X, Y), f32),
        ),
        in_specs=[vmem, vmem],
        out_specs=(hbm, hbm),
        scratch_shapes=[pltpu.SemaphoreType.DMA((2,))],
        compiler_params=pltpu.CompilerParams(vmem_limit_bytes=2 * 2**20),
    )(corrected, images)
    return corrected.reshape(3, Z, X, Y), images.reshape(1, 4, X, Y)


def solution(mesh):
    sizes = (mesh.shape["gx"], mesh.shape["gy"], mesh.shape["gz"])
    return jax.shard_map(
        functools.partial(local, sizes),
        mesh=mesh,
        in_specs=(
            P("gz", "gx", "gy"),
            P("gz", "gx", "gy"),
            P(None, "gz", "gx", "gy"),
            P(),
            P(),
            P(),
        ),
        out_specs=(P(None, "gz", "gx", "gy"), P("gz", None, "gx", "gy")),
        check_vma=False,
    )
```

```python
import functools

import jax
import jax.numpy as jnp
from jax import lax
from jax.experimental import pallas as pl
from jax.experimental.pallas import tpu as pltpu
from jax.sharding import PartitionSpec as P

MESH = pl.DeviceIdType.MESH
Z, X, Y = 8, 16, 128
R = Z * X
K = R // 8
TF = 8
PAD = 8
FAR_FIRST = (4, 3, 5, 2, 6, 1, 7)


def lanes(shape):
    return lax.broadcasted_iota(jnp.int32, shape, 1)


def group(v, k):
    return v[8 * k : 8 * k + 8]


def recip(v):
    r = pl.reciprocal(v, approx=True)
    r = r * (2.0 - v * r)
    return r * (2.0 - v * r)


def pack_ends(v):
    lane = lanes((8, Y))
    out = jnp.zeros((8, Y), jnp.float32)
    for k in range(K):
        out = jnp.where(lane // 2 == k, pltpu.roll(group(v, k), 2 * k + 1, 1), out)
    return out


def merge(below, above):
    even = lanes((8, Y)) % 2 == 0
    return jnp.where(even, pltpu.roll(above, Y - 1, 1), pltpu.roll(below, 1, 1))


def unpack(both):
    return jnp.concatenate([pltpu.roll(both, Y - (2 * k + 1), 1) for k in range(K)], axis=0)


def rows_of(first, second):
    return jnp.concatenate(
        [jnp.broadcast_to(first, (8, Y)), jnp.broadcast_to(second, (8, Y))], axis=0
    )


def spread(below, above):
    pieces = []
    for z in range(Z):
        pieces.append(jnp.broadcast_to(below[z : z + 1], (8, Y)))
        pieces.append(jnp.broadcast_to(above[z : z + 1], (8, Y)))
    return jnp.concatenate(pieces, axis=0)


def kernel(
    sizes,
    phase_in,
    thermal_in,
    vel_in,
    slope_in,
    offset_in,
    gain_in,
    corrected,
    images,
    slope,
    offset,
    gain,
    phase_v,
    thermal_v,
    vel_v,
    vel1_pad,
    den_pad,
    s1z,
    s1x,
    s1xu,
    s1y,
    h1,
    v_pad,
    coef,
    edge_z,
    weights,
    stat_z,
    stat_x,
    stat_y,
    stat,
    stat_m,
    scaled_v,
    dz,
    dx,
    dy,
    h,
    grads,
    row_send,
    row_plane,
    row_line,
    send_a,
    send_c,
    recv_a,
    recv_c,
    vel_sum,
    img_send,
    img_recv,
    in_sem,
    send_sem,
    recv_sem,
    known,
):
    nx, ny, nz = sizes
    ix, iy, iz = lax.axis_index("gx"), lax.axis_index("gy"), lax.axis_index("gz")
    xm, xp = {"gx": lax.rem(ix + nx - 1, nx)}, {"gx": lax.rem(ix + 1, nx)}
    ym, yp = {"gy": lax.rem(iy + ny - 1, ny)}, {"gy": lax.rem(iy + 1, ny)}
    zm, zp = {"gz": lax.rem(iz + nz - 1, nz)}, {"gz": lax.rem(iz + 1, nz)}
    x_first, x_last = ix == 0, ix == nx - 1
    y_first, y_last = iy == 0, iy == ny - 1
    z_first, z_last = iz == 0, iz == nz - 1

    loads = [
        pltpu.make_async_copy(phase_in, phase_v, in_sem.at[0]),
        pltpu.make_async_copy(thermal_in, thermal_v, in_sem.at[1]),
    ] + [
        pltpu.make_async_copy(
            vel_in.at[pl.ds(d * R, R)], vel_v.at[pl.ds(d * R, R)], in_sem.at[6 + d]
        )
        for d in range(3)
    ]
    params = [
        pltpu.make_async_copy(slope_in, slope, in_sem.at[3]),
        pltpu.make_async_copy(offset_in, offset, in_sem.at[4]),
        pltpu.make_async_copy(gain_in, gain, in_sem.at[5]),
    ]
    for copy in loads:
        copy.start()
    barrier = pltpu.get_barrier_semaphore()
    for device in (zm, zp, ym, yp, xm, xp):
        pl.semaphore_signal(barrier, inc=1, device_id=device, device_id_type=MESH)
    for copy in params:
        copy.start()

    pad = jnp.zeros((PAD, Y), jnp.float32)
    for ref in [den_pad, vel1_pad] + [v_pad.at[j] for j in range(4)]:
        ref[0:PAD] = pad
        ref[PAD + R : PAD + R + PAD] = pad

    def send(src, dst, group_id, device):
        pltpu.make_async_remote_copy(
            src, dst, send_sem.at[group_id], recv_sem.at[group_id], device_id=device, device_id_type=MESH
        ).start()

    def whole(ref, group_id):
        return pltpu.make_async_remote_copy(
            ref, ref, send_sem.at[group_id], recv_sem.at[group_id], device_id=xp, device_id_type=MESH
        )

    def in_plane(dx, dy):
        return {"gx": lax.rem(ix + dx, nx), "gy": lax.rem(iy + dy, ny)}

    def hello(which, dx, dy):
        pl.semaphore_signal(
            known.at[which], inc=1, device_id=in_plane(dx, dy), device_id_type=MESH
        )

    lane = lanes((R, Y))
    row = lax.broadcasted_iota(jnp.int32, (R, Y), 0)
    in_x = row % X

    for copy in loads[:2]:
        copy.wait()
    den = (1.0 + 9.0 * phase_v[...].astype(jnp.float32)) * thermal_v[...]
    den_pad[PAD : PAD + R] = den
    s1xu[...] = den_pad[pl.ds(PAD + X - 1, 8, stride=X)]
    ends = pack_ends(den)
    for copy in loads[2:]:
        copy.wait()
    vel0, vel1, vel2 = vel_v[0:R], vel_v[R : 2 * R], vel_v[2 * R : 3 * R]
    vel1_pad[PAD : PAD + R] = vel1
    s1z[0:X] = den[0:X]
    s1z[X : 2 * X] = vel0[0:X]
    s1x[0:8] = den_pad[pl.ds(PAD, 8, stride=X)]
    s1x[8:16] = vel1_pad[pl.ds(PAD, 8, stride=X)]
    lane8 = lanes((8, Y))
    for k in range(K):
        ends = jnp.where(lane8 == 2 * K + k, pltpu.roll(group(vel2, k), 2 * K + k, 1), ends)
    s1y[...] = ends

    pl.semaphore_wait(barrier, 6)

    send(den_pad.at[pl.ds(PAD + R - X, X)], h1.at[pl.ds(0, 16)], 0, zp)
    send(s1z, h1.at[pl.ds(16, 32)], 0, zm)
    send(s1xu, h1.at[pl.ds(48, 8)], 0, xp)
    send(s1x, h1.at[pl.ds(56, 16)], 0, xm)
    send(s1y, h1.at[pl.ds(72, 8)], 0, yp)
    send(s1y, h1.at[pl.ds(80, 8)], 0, ym)
    whole(h1, 0).wait_recv()
    wide = nx == 8 and ny == 8
    if wide:
        for far in ((2, 0), (6, 0), (0, 2), (0, 6)):
            hello(0, *far)
    for step in (2, 6):
        pl.semaphore_signal(
            known.at[2], inc=1, device_id={"gz": lax.rem(iz + step, nz)}, device_id_type=MESH
        )

    def face(first, own, other):
        return jnp.where(first, own, other)

    zb = jnp.concatenate([face(z_first, den[0:X], h1[0:16]), den[: R - X]], axis=0)
    za = jnp.concatenate([den[X:], face(z_last, den[R - X :], h1[16:32])], axis=0)
    bx = spread(h1[48:56], h1[56:64])
    xb = jnp.where(in_x == 0, face(x_first, den, bx), den_pad[PAD - 1 : PAD - 1 + R])
    xa = jnp.where(in_x == X - 1, face(x_last, den, bx), den_pad[PAD + 1 : PAD + 1 + R])
    by = unpack(merge(h1[72:80], h1[80:88]))
    yb = jnp.where(lane == 0, face(y_first, den, by), pltpu.roll(den, 1, 1))
    ya = jnp.where(lane == Y - 1, face(y_last, den, by), pltpu.roll(den, Y - 1, 1))
    low_z = 2.0 * recip(den + zb)
    up_z = jnp.concatenate([low_z[X:], 2.0 * recip(den[R - X :] + za[R - X :])], axis=0)
    low_x, up_x = 2.0 * recip(den + xb), 2.0 * recip(den + xa)
    low_y, up_y = 2.0 * recip(den + yb), 2.0 * recip(den + ya)
    inverse = recip(low_z + up_z + low_x + up_x + low_y + up_y)

    def keep(flag):
        return jnp.where(flag, 0.0, 1.0)

    zero = jnp.zeros((R, Y), jnp.float32)
    coef[0] = low_z
    coef[1] = low_x
    coef[2] = low_y
    coef[3] = up_z
    coef[4] = jnp.where(in_x == X - 1, 0.0, up_x)
    coef[5] = jnp.where(lane == Y - 1, 0.0, up_y)
    coef[6] = jnp.where(in_x == 0, 0.0, low_x)
    coef[7] = jnp.where(lane == 0, 0.0, low_y)
    coef[8] = jnp.where(
        in_x == 0, low_x * keep(x_first), jnp.where(in_x == X - 1, up_x * keep(x_last), zero)
    )
    coef[9] = jnp.where(
        lane == 0, low_y * keep(y_first), jnp.where(lane == Y - 1, up_y * keep(y_last), zero)
    )
    coef[10] = inverse
    edge_z[0:X] = low_z[0:X] * keep(z_first)
    edge_z[X : 2 * X] = up_z[R - X :] * keep(z_last)

    weights[0] = inverse * coef[8]
    weights[1] = inverse * coef[9]
    weights[2] = zero
    weights[2, 0:X] = inverse[0:X] * edge_z[0:X]
    weights[2, R - X : R] = inverse[R - X :] * edge_z[X : 2 * X]
    for i in range(3):
        stat_z[0, 16 * i : 16 * i + 16] = weights[i, 0:X]
        stat_z[1, 16 * i : 16 * i + 16] = weights[i, R - X : R]
        face_x = weights.at[i]
        stat_x[0, 8 * i : 8 * i + 8] = face_x[pl.ds(0, 8, stride=X)]
        stat_x[1, 8 * i : 8 * i + 8] = face_x[pl.ds(X - 1, 8, stride=X)]
        stat_y[8 * i : 8 * i + 8] = pack_ends(weights[i])
    send(stat_z.at[1], stat.at[pl.ds(0, 48)], 3, zp)
    send(stat_z.at[0], stat.at[pl.ds(48, 48)], 3, zm)
    send(stat_y, stat.at[pl.ds(96, 24)], 3, yp)
    send(stat_y, stat.at[pl.ds(120, 24)], 3, ym)
    send(stat_x.at[1], stat.at[pl.ds(144, 24)], 3, xp)
    send(stat_x.at[0], stat.at[pl.ds(168, 24)], 3, xm)

    above0 = jnp.concatenate([vel0[X:], h1[32:48] * keep(z_last)], axis=0)
    bv = spread(h1[56:64], h1[64:72])
    above1 = jnp.where(in_x == X - 1, bv * keep(x_last), vel1_pad[PAD + 1 : PAD + 1 + R])
    ends_above = h1[80:88]
    bw = jnp.concatenate(
        [pltpu.roll(ends_above, Y - 1 - (2 * K + k), 1) for k in range(K)], axis=0
    )
    above2 = jnp.where(lane == Y - 1, bw * keep(y_last), pltpu.roll(vel2, Y - 1, 1))
    rhs = -(((above0 - vel0) + (above1 - vel1)) + (above2 - vel2))

    def hand_out(buf, recv, group_id, steps):
        rows = buf.shape[1]
        for k in steps:
            to = lax.rem(iz + k, nz)
            send(buf.at[to], recv.at[pl.ds(iz * rows, rows)], group_id, {"gz": to})

    def scatter(fields, buf, recv, group_id, steps):
        for q, ref in enumerate(fields):
            for t in range(TF):
                for r in range(2):
                    at = 16 * q + 8 * r
                    buf[t, at : at + 8] = ref[pl.ds(r * (R // 2) + t, 8, stride=8)]
        rows = 16 * len(fields)
        hand_out(buf, recv, group_id, steps)
        recv[pl.ds(pl.multiple_of(iz * rows, rows), rows)] = buf[iz]

    folded = []

    def fold(value):
        value = jnp.sum(value.reshape(K, 8, Y), axis=0)
        for step in (64, 32, 16):
            value = value + pltpu.roll(value, step, 1)
        m = len(folded)
        before = folded[-1] if folded else jnp.zeros((8, Y), jnp.float32)
        folded.append(jnp.where(lane8 // 16 == m, value, before))

    def gradient(j, v, z_low, x_low, y_low):
        g0, g1, g2 = coef[0] * v - z_low, coef[1] * v - x_low, coef[2] * v - y_low
        grads[j, 0] = g0
        grads[j, 1] = g1
        grads[j, 2] = g2
        grads[j, 3] = g0 + g1 + g2

    def near(axis, here, count, step):
        return {axis: lax.rem(here + count - step, count)}

    edges = (4, 3)
    waits = [pl.ds(0, 128 + 25 * count) for count in edges]

    def exchange(p, own, v, inner):
        nxt = coef[10] * inner
        scaled_v[p] = nxt
        hp = h.at[p]
        for side, at in ((1, R - X), (0, 0)):
            dz[p, side, 0:16] = v[at : at + X]
            dz[p, side, 16:32] = nxt[at : at + X]
        q = pack_ends(v)
        dy[p, 0:8] = q
        dy[p, 8:16] = pack_ends(nxt)
        for side, at in ((1, X - 1), (0, 0)):
            dx[p, side, 0:8] = scaled_v.at[p][pl.ds(at, 8, stride=X)]
            dx[p, side, 8:16] = own[pl.ds(PAD + at, 8, stride=X)]
            dx[p, side, 16:24] = q
        signs = ((-1, -1), (-1, 1), (1, -1), (1, 1))[: edges[p]]
        for i, (a, b) in enumerate(signs):
            to = near("gz", iz, nz, a) | near("gy", iy, ny, b)
            send(dy.at[p, pl.ds(0, 8)], hp.at[pl.ds(128 + 8 * i, 8)], 1 + p, to)
        for i, (a, b) in enumerate(signs):
            to = near("gx", ix, nx, a) | near("gy", iy, ny, b)
            side = 1 if a < 0 else 0
            send(dx.at[p, side, pl.ds(8, 16)], hp.at[pl.ds(160 + 16 * i, 16)], 1 + p, to)
        for i, (a, b) in enumerate(signs):
            row_at = PAD + (R - X if a < 0 else 0) + (X - 1 if b < 0 else 0)
            to = near("gz", iz, nz, a) | near("gx", ix, nx, b)
            send(own.at[pl.ds(row_at, 1)], hp.at[pl.ds(224 + i, 1)], 1 + p, to)
        send(dz.at[p, 1], hp.at[pl.ds(0, 32)], 1 + p, zp)
        send(dz.at[p, 0], hp.at[pl.ds(32, 32)], 1 + p, zm)
        send(dy.at[p], hp.at[pl.ds(96, 16)], 1 + p, yp)
        send(dy.at[p], hp.at[pl.ds(112, 16)], 1 + p, ym)
        send(dx.at[p, 1, pl.ds(0, 16)], hp.at[pl.ds(64, 16)], 1 + p, xp)
        send(dx.at[p, 0, pl.ds(0, 16)], hp.at[pl.ds(80, 16)], 1 + p, xm)

    sub8 = lax.broadcasted_iota(jnp.int32, (8, Y), 0)

    def received(p):
        hp = h.at[p]
        z_faces = (hp[0:16], hp[32:48])
        x_faces = (hp[72:80], hp[88:96])
        return z_faces, x_faces, merge(hp[96:104], hp[112:120])

    def computed(p, v):
        hp = h.at[p]
        low_only = p == 1
        pairs = ((0, 1), (2, 2 if low_only else 3))
        corner = [[hp[224 + i : 225 + i] for i in pair] for pair in pairs]
        zy = [merge(*(hp[128 + 8 * i : 136 + 8 * i] for i in pair)) for pair in pairs]
        xy_rows = [[hp[160 + 16 * i : 168 + 16 * i] for i in pair] for pair in pairs]
        xy = [merge(*(hp[168 + 16 * i : 176 + 16 * i] for i in pair)) for pair in pairs]
        z_faces, x_faces = [], []
        for a, (at, first) in enumerate(((0, 2 * K - 4), (R - X, 0))[: 2 - low_only]):
            from_y = jnp.concatenate(
                [pltpu.roll(zy[a], Y - first - 1, 1), pltpu.roll(zy[a], Y - first - 3, 1)], axis=0
            )
            value = hp[16 + 32 * a : 32 + 32 * a]
            value = value + stat[48 * a + 32 : 48 * a + 48] * v[at : at + X]
            value = value + stat[48 * a : 48 * a + 16] * rows_of(corner[a][0], corner[a][1])
            z_faces.append(value + stat[48 * a + 16 : 48 * a + 32] * from_y)
        for a in range(2 - low_only):
            mine = dx[p, a, 8:16]
            from_z = jnp.where(
                sub8 == 0,
                jnp.broadcast_to(corner[0][a], (8, Y)),
                jnp.broadcast_to(corner[1][a], (8, Y)),
            )
            from_y = jnp.where(
                lane8 == 0, pltpu.roll(xy_rows[a][0], 1, 1), pltpu.roll(xy_rows[a][1], Y - 1, 1)
            )
            at = 144 + 24 * a
            value = hp[64 + 16 * a : 72 + 16 * a] + stat[at : at + 8] * mine
            value = value + stat[at + 8 : at + 16] * from_y
            x_faces.append(value + stat[at + 16 : at + 24] * from_z)
        last_z = 2 * K - 4
        from_z = jnp.where(lane8 < 4, pltpu.roll(zy[0], Y - last_z, 1), pltpu.roll(zy[1], last_z, 1))
        from_x = jnp.where(
            sub8 == 0,
            pltpu.roll(pltpu.roll(xy[0], Y - 2, 1), 1, 0),
            pltpu.roll(pltpu.roll(xy[1], 2, 1), 7, 0),
        )
        both = merge(hp[104:112], hp[120:128])
        both = both + stat_m[8:16] * dy[p, 0:8]
        both = both + stat_m[0:8] * from_x
        return z_faces, x_faces, both + stat_m[16:24] * from_z

    vel_sum[...] = vel0 + vel1 + vel2
    scaled = rhs
    late = None
    for j in range(4):
        p = j // 2
        v = coef[10] * scaled
        own = v_pad.at[j]
        own[PAD : PAD + R] = v
        z_low = coef[0, X:R] * v[: R - X]
        x_low = coef[6] * own[PAD - 1 : PAD - 1 + R]
        y_low = coef[7] * pltpu.roll(v, 1, 1)
        if j < 3:
            z_up = coef[3, 0 : R - X] * v[X:]
            x_up = coef[4] * own[PAD + 1 : PAD + 1 + R]
            y_up = coef[5] * pltpu.roll(v, Y - 1, 1)
            rest = (x_low + x_up) + (y_low + y_up)
        if j % 2 == 0:
            edge = jnp.zeros((X, Y), jnp.float32)
            inner = jnp.concatenate([edge, z_low], axis=0) + jnp.concatenate([z_up, edge], axis=0)
            exchange(p, own, v, inner + rest)
            earlier = late
            if j:
                step_v = last[0] - v
                fold(last[5] * step_v)
                fold(last[4] * step_v)
                gradient(*earlier)
                gradient(1, *last[:4])
                scatter([vel_sum, grads.at[0, 3], grads.at[1, 3]], send_a, recv_a, 8, FAR_FIRST)
            if j == 0:
                fold(scaled * v)
                if wide:
                    pl.semaphore_wait(known.at[0], 4)
                pl.semaphore_wait(known.at[2], 2)
                whole(stat, 3).wait_recv()
                for i in range(3):
                    stat_m[8 * i : 8 * i + 8] = merge(
                        stat[96 + 8 * i : 104 + 8 * i], stat[120 + 8 * i : 128 + 8 * i]
                    )
            elif wide:
                pl.semaphore_wait(known.at[1], 2)
            whole(h.at[p, waits[p]], 1 + p).wait_recv()
            if wide and j == 0:
                hello(1, 4, 0)
                hello(1, 0, 4)
            z_faces, x_faces, both = received(p)
        else:
            step_v = prior[0] - v
            fold(prior[1] * step_v)
            fold(scaled * step_v)
            z_faces, x_faces, both = following
        z_low = jnp.concatenate([edge_z[0:X] * z_faces[0], z_low], axis=0)
        x_edge = coef[8] * spread(x_faces[0], x_faces[-1])
        y_edge = coef[9] * unpack(both)
        x_low = x_low + jnp.where(in_x == 0, x_edge, 0.0)
        y_low = y_low + jnp.where(lane == 0, y_edge, 0.0)
        prior = (v, scaled)
        if j < 3:
            z_up = jnp.concatenate([z_up, edge_z[X : 2 * X] * z_faces[1]], axis=0)
            scaled = ((z_low + z_up) + rest) + (x_edge + y_edge)
        if j % 2 == 0:
            following = computed(p, v)
            late = (j, v, z_low, x_low, y_low)
        elif j == 1:
            last = (v, z_low, x_low, y_low, scaled, prior[1])
        else:
            fold(v * (scaled - 2.0 * ((z_low + x_low) + y_low)))

    line = jnp.sum(folded[-1], axis=0, keepdims=True)
    row_send[0] = line
    others = [(dx, dy) for dx in range(nx) for dy in range(ny) if dx or dy]

    others.sort(key=lambda apart: ((apart[1] - 1) % ny, -min(apart[0], nx - apart[0])))
    for at, apart in enumerate(others):
        send(row_send.at[0], row_plane.at[pl.ds(at, 1)], 5, in_plane(*apart))
    row_plane[pl.ds(len(others), 1)] = line
    gradient(*late)
    gradient(3, v, z_low, x_low, y_low)
    scatter([grads.at[2, 3], grads.at[3, 3]], send_c, recv_c, 10, FAR_FIRST)
    whole(row_plane.at[pl.ds(0, len(others))], 5).wait_recv()
    line = jnp.sum(row_plane[0 : len(others) + 1], axis=0, keepdims=True)
    row_send[1] = line
    for k in FAR_FIRST:
        send(row_send.at[1], row_line.at[pl.ds(k - 1, 1)], 6, {"gz": lax.rem(iz + k, nz)})
    row_line[nz - 1 : nz] = line
    for ref, group_id in ((recv_a, 8), (recv_c, 10)):
        whole(ref.at[pl.ds(0, ref.shape[0] // nz * (nz - 1))], group_id).wait_recv()
    for copy in params:
        copy.wait()
    whole(row_line.at[pl.ds(0, nz - 1)], 6).wait_recv()
    line = jnp.sum(row_line[...], axis=0, keepdims=True)
    lane1 = lanes((1, Y))
    m = [jnp.sum(jnp.where(lane1 // 16 == i, line, 0.0), axis=1, keepdims=True) for i in range(8)]

    drop = m[1:]
    a = [[drop[i + j] for j in range(4)] for i in range(4)]
    b = [m[0]]
    for i in range(3):
        b.append(b[i] - drop[i])
    pivots = []
    for p in range(4):
        ok = a[p][p] > 1e-7 * drop[2 * p]
        pivots.append(jnp.where(ok, 1.0 / jnp.where(ok, a[p][p], 1.0), 0.0))
        for i in range(p + 1, 4):
            factor = a[p][i] * pivots[p]
            for j in range(i, 4):
                a[i][j] = a[i][j] - factor * a[p][j]
            b[i] = b[i] - factor * b[p]
    c = [None] * 4
    for p in reversed(range(4)):
        value = b[p]
        for j in range(p + 1, 4):
            value = value - a[p][j] * c[j]
        c[p] = value * pivots[p]

    field = []
    for z in range(Z):
        halves = []
        for r in range(2):
            at = 2 * z + r
            value = recv_a[pl.ds(at, 8, stride=48)]
            value = value - c[0] * recv_a[pl.ds(16 + at, 8, stride=48)]
            value = value - c[1] * recv_a[pl.ds(32 + at, 8, stride=48)]
            value = value - c[2] * recv_c[pl.ds(at, 8, stride=32)]
            value = value - c[3] * recv_c[pl.ds(16 + at, 8, stride=32)]
            halves.append(value)
        field.append(jnp.concatenate(halves, axis=0))
    sub = lax.broadcasted_iota(jnp.int32, (8, Y), 0)
    for k in FAR_FIRST + (0,):
        t = lax.rem(iz + k, nz)
        half = 0.5 / (Z * nz) * gain[t]
        slopes = [0.5 * slope[i, t] for i in range(4)]
        offsets = [0.5 * offset[i, t] for i in range(4)]
        through = jnp.ones((16, Y), jnp.float32)
        colors = [jnp.zeros((16, Y), jnp.float32) for _ in range(3)]
        for z in range(Z):
            weight = through * (half + half * jnp.tanh(slopes[3] * field[z] + offsets[3]))
            through = through - weight
            for i in range(3):
                colors[i] = colors[i] + weight * jnp.tanh(slopes[i] * field[z] + offsets[i])
        lines = [[None, None] for _ in range(4)]
        for r in range(2):
            here = through[8 * r : 8 * r + 8]
            before = jnp.where(sub >= 1, pltpu.roll(here, 1, 0), 1.0)
            for step in (1, 2, 4):
                before = before * jnp.where(sub >= step, pltpu.roll(before, step, 0), 1.0)
            for i in range(3):
                color = 0.5 * (colors[i][8 * r : 8 * r + 8] + (1.0 - here))
                lines[i][r] = jnp.sum(before * color, axis=0, keepdims=True)
            lines[3][r] = (1.0 - before * here)[7:8]
        tile = jnp.concatenate([lines[i][r] for i in range(4) for r in range(2)], axis=0)
        if k:
            img_send[t] = tile
            send(img_send.at[t], img_recv.at[pl.ds(iz * 8, 8)], 11, {"gz": t})
        else:
            img_recv[pl.ds(pl.multiple_of(iz * 8, 8), 8)] = tile
    for d in range(3):
        value = vel_v[d * R : (d + 1) * R]
        for j in range(4):
            value = value - c[j] * grads[j, d]
        corrected[d * R : (d + 1) * R] = value
    whole(h1, 0).wait_send()
    whole(stat, 3).wait_send()
    for p in range(2):
        whole(h.at[p, waits[p]], 1 + p).wait_send()
    whole(row_plane.at[pl.ds(0, len(others))], 5).wait_send()
    whole(row_line.at[pl.ds(0, nz - 1)], 6).wait_send()
    for ref, group_id in ((recv_a, 8), (recv_c, 10)):
        whole(ref.at[pl.ds(0, ref.shape[0] // nz * (nz - 1))], group_id).wait_send()
    whole(img_recv.at[pl.ds(0, 8 * (nz - 1))], 11).wait_recv()
    whole(img_recv.at[pl.ds(0, 8 * (nz - 1))], 11).wait_send()
    for i in range(4):
        for r in range(2):
            images[i * X + 8 * r : i * X + 8 * r + 8] = img_recv[pl.ds(2 * i + r, 8, stride=8)]


def write_out(corrected, images, corrected_out, images_out, sem):
    copies = [
        pltpu.make_async_copy(corrected, corrected_out, sem.at[0]),
        pltpu.make_async_copy(images, images_out, sem.at[1]),
    ]
    for copy in copies:
        copy.start()
    for copy in copies:
        copy.wait()


def local(sizes, phase_field, thermal, velocity, transfer_slope, transfer_offset, transfer_gain):
    f32 = jnp.float32
    hbm = pl.BlockSpec(memory_space=pltpu.HBM)
    vmem = pl.BlockSpec(memory_space=pltpu.VMEM)
    corrected, images = pl.pallas_call(
        functools.partial(kernel, sizes),
        out_shape=(
            jax.ShapeDtypeStruct((3 * R, Y), f32),
            jax.ShapeDtypeStruct((4 * X, Y), f32),
        ),
        in_specs=[hbm] * 6,
        out_specs=(vmem, vmem),
        scratch_shapes=[
            pltpu.SMEM((4, TF), f32),
            pltpu.SMEM((4, TF), f32),
            pltpu.SMEM((TF,), f32),
            pltpu.VMEM((R, Y), jnp.int32),
            pltpu.VMEM((R, Y), f32),
            pltpu.VMEM((3 * R, Y), f32),
            pltpu.VMEM((R + 2 * PAD, Y), f32),
            pltpu.VMEM((R + 2 * PAD, Y), f32),
            pltpu.VMEM((2 * X, Y), f32),
            pltpu.VMEM((16, Y), f32),
            pltpu.VMEM((8, Y), f32),
            pltpu.VMEM((8, Y), f32),
            pltpu.VMEM((88, Y), f32),
            pltpu.VMEM((4, R + 2 * PAD, Y), f32),
            pltpu.VMEM((11, R, Y), f32),
            pltpu.VMEM((2 * X, Y), f32),
            pltpu.VMEM((3, R, Y), f32),
            pltpu.VMEM((2, 48, Y), f32),
            pltpu.VMEM((2, 24, Y), f32),
            pltpu.VMEM((24, Y), f32),
            pltpu.VMEM((192, Y), f32),
            pltpu.VMEM((24, Y), f32),
            pltpu.VMEM((2, R, Y), f32),
            pltpu.VMEM((2, 2, 32, Y), f32),
            pltpu.VMEM((2, 2, 24, Y), f32),
            pltpu.VMEM((2, 16, Y), f32),
            pltpu.VMEM((2, 232, Y), f32),
            pltpu.VMEM((4, 4, R, Y), f32),
            pltpu.VMEM((2, 1, Y), f32),
            pltpu.VMEM((sizes[0] * sizes[1], Y), f32),
            pltpu.VMEM((sizes[2], Y), f32),
            pltpu.VMEM((TF, 48, Y), f32),
            pltpu.VMEM((TF, 32, Y), f32),
            pltpu.VMEM((TF * 48, Y), f32),
            pltpu.VMEM((TF * 32, Y), f32),
            pltpu.VMEM((R, Y), f32),
            pltpu.VMEM((TF, 8, Y), f32),
            pltpu.VMEM((TF * 8, Y), f32),
            pltpu.SemaphoreType.DMA((9,)),
            pltpu.SemaphoreType.DMA((12,)),
            pltpu.SemaphoreType.DMA((12,)),
            pltpu.SemaphoreType.REGULAR((3,)),
        ],
        compiler_params=pltpu.CompilerParams(
            collective_id=0, has_side_effects=True, vmem_limit_bytes=16 * 2**20
        ),
    )(
        *(
            pltpu.with_memory_space_constraint(value, pltpu.HBM)
            for value in (
                phase_field.reshape(R, Y),
                thermal.reshape(R, Y),
                velocity.reshape(3 * R, Y),
                transfer_slope.T,
                transfer_offset.T,
                transfer_gain,
            )
        )
    )
    corrected, images = pl.pallas_call(
        write_out,
        out_shape=(
            jax.ShapeDtypeStruct((3 * R, Y), f32),
            jax.ShapeDtypeStruct((4 * X, Y), f32),
        ),
        in_specs=[vmem, vmem],
        out_specs=(hbm, hbm),
        scratch_shapes=[pltpu.SemaphoreType.DMA((2,))],
        compiler_params=pltpu.CompilerParams(vmem_limit_bytes=2 * 2**20),
    )(corrected, images)
    return corrected.reshape(3, Z, X, Y), images.reshape(1, 4, X, Y)


def solution(mesh):
    sizes = (mesh.shape["gx"], mesh.shape["gy"], mesh.shape["gz"])
    return jax.shard_map(
        functools.partial(local, sizes),
        mesh=mesh,
        in_specs=(
            P("gz", "gx", "gy"),
            P("gz", "gx", "gy"),
            P(None, "gz", "gx", "gy"),
            P(),
            P(),
            P(),
        ),
        out_specs=(P(None, "gz", "gx", "gy"), P("gz", None, "gx", "gy")),
        check_vma=False,
    )
```
